128 devices in a mesh: seq: 32 (over z, x, core), head: 4 (over y).
Axes of the slice: x: 4, y: 4, z: 4, core: 2. Of those that a mesh axis runs over, the one named last changes fastest.
Arguments:
- queries: bfloat16 [16384, 4096], P('seq', 'head'), may hold values from -6 to 6
- keys: bfloat16 [16384, 4096], P('seq', 'head'), may hold values from -0.625 to 0.625
- values: bfloat16 [16384, 4096], P('seq', 'head'), may hold values from -6 to 6
- logdecay: float32 [16384, 32], P('seq', 'head'), may hold values from -1 to 0
- out_weight: bfloat16 [4096, 6144], P('head'), may hold values from -0.09375 to 0.09375
- output_gradient: bfloat16 [16384, 6144], P('seq', 'head'), may hold values from -6 to 6
Outputs:
- attn_out: bfloat16 [16384, 6144], P('seq', 'head')
- grad_queries: bfloat16 [16384, 4096], P('seq', 'head')
- grad_keys: bfloat16 [16384, 4096], P('seq', 'head')
- grad_values: bfloat16 [16384, 4096], P('seq', 'head')
The draws below stay inside these ranges and needn't reach their ends.
All inputs are finite; a program needn't handle non-finite values.
Results may differ from the reference program's by a relative error of at most 0.018.
Values may be sent and summed in bfloat16 or wider, within the bound.
No kernel may reach another device: no remote copies, remote signals or barrier semaphores. Data moves between devices by JAX's collectives and lax.ppermute only.
A program may use at most 192 MiB of HBM per device.

```python
import math
import jax
import jax.numpy as jnp
from jax import lax

D = 6144
H = 32
HD = 128
TOK_DEV = 512
TOKENS = 16384


def draw_logdecay(key, part):
    key = jax.random.fold_in(key, 7)
    every_key_row = jax.random.split(key, 7)
    fast_share = 0.5
    pick = jax.random.uniform(every_key_row[0], (H,))
    fast_rate = jnp.exp(jax.random.uniform(every_key_row[1], (H,), minval=math.log(1.0 / 50.0), maxval=math.log(1.0 / 30.0)))
    slow_rate = jnp.exp(jax.random.uniform(every_key_row[2], (H,), minval=math.log(0.1), maxval=math.log(0.6))) / TOKENS
    rate = jnp.where(pick < fast_share, fast_rate, slow_rate)
    count = TOKENS // TOK_DEV
    device_factor = jnp.exp(jax.random.uniform(every_key_row[3], (count, 1, H), minval=math.log(0.5), maxval=math.log(1.5)))
    rough = jax.random.uniform(every_key_row[4], (count, TOK_DEV, H), minval=0.5, maxval=1.5)
    constant_level = (rate[None, None, :] * device_factor * rough).reshape(TOKENS, H)
    places = jax.random.randint(every_key_row[5], (2,), 0, TOKENS)
    retained_part = jax.random.uniform(every_key_row[6], (2, H), minval=0.5, maxval=0.8)
    position = jnp.arange(TOKENS)[:, None, None]
    match_tally = (position == places[None, None, :]).astype(jnp.float32)
    sudden_jumps = jnp.sum(match_tally * jnp.log(retained_part).T[None, :, :], axis=-1)
    return (sudden_jumps - constant_level).astype(jnp.float32)


def shard_levels(stream_key, shape, pieces, low, largest):
    factor_of = 1.0
    for axis_at, blocks in pieces:
        heights = jax.random.uniform(jax.random.fold_in(jax.random.fold_in(stream_key, 6), axis_at), (blocks,), jnp.float32, low / len(pieces), largest / len(pieces))
        factor_of = factor_of * jnp.repeat(jnp.exp(heights), shape[axis_at] // blocks).reshape((-1,) + (1,) * (len(shape) - 1 - axis_at))
    return factor_of


def normal_values(own_key, extent, spread, reach, shards=(), dtype=jnp.bfloat16):
    drawn = spread * jax.random.normal(own_key, extent, jnp.float32)
    if shards:
        drawn = drawn * shard_levels(own_key, extent, shards, -0.22, 0.18)
    return jnp.clip(drawn, -reach, reach).astype(dtype)


def setup_inputs(seed: int = 0) -> dict:
    key_list = jax.random.split(jax.random.key(seed), 7)
    return {
        "queries": normal_values(key_list[0], (TOKENS, H * HD), 1.0, 6.0, ((0, 32), (1, 4))),
        "keys": normal_values(key_list[1], (TOKENS, H * HD), 0.1, 0.625, ((0, 32), (1, 4))),
        "values": normal_values(key_list[2], (TOKENS, H * HD), 1.0, 6.0, ((0, 32), (1, 4))),
        "logdecay": draw_logdecay(jax.random.fold_in(key_list[6], 71), 0),
        "out_weight": normal_values(key_list[4], (H * HD, D), (H * HD) ** -0.5, 0.09375, ((0, 4),)),
        "output_gradient": normal_values(key_list[5], (TOKENS, D), 1.0, 6.0, ((0, 32), (1, 4))),
    }


EPS = 1e-05

def decay_lookup_grid(cum_decay):
    along = cum_decay.T
    diff = along[:, :, None] - along[:, None, :]
    rows = cum_decay.shape[0]
    later = lax.broadcasted_iota(jnp.int32, (rows, rows), 0) >= lax.broadcasted_iota(jnp.int32, (rows, rows), 1)
    return jnp.exp(jnp.where(later[None], diff, -1e+30))

def head_norm(attention):
    return attention * lax.rsqrt(lax.optimization_barrier(jnp.mean(attention * attention, axis=-1, keepdims=True)) + EPS)

def mix(form, left, right):
    return jnp.einsum(form, left.astype(jnp.float32), right.astype(jnp.float32), precision=lax.Precision.HIGHEST)

def reference(queries, keys, values, logdecay, out_weight, output_gradient):
    count = TOKENS // TOK_DEV
    shape = (count, TOK_DEV, H, HD)
    query_blocks = queries.reshape(shape)
    key_blocks = keys.reshape(shape)
    value_blocks = values.reshape(shape)
    decay_blocks = logdecay.reshape(count, TOK_DEV, H)

    def forward_step(state, inputs):
        head_query, head_key, head_value, decay = inputs
        cum_decay = jnp.cumsum(decay, axis=0)
        block_decay = cum_decay[-1]
        table = decay_lookup_grid(cum_decay)
        probs = (mix('thd,shd->hts', head_query, head_key) * table).astype(jnp.bfloat16)
        local = mix('hts,she->the', probs, head_value)
        scaled_query = head_query.astype(jnp.float32) * jnp.exp(cum_decay)[:, :, None]
        attention = local + mix('thd,hde->the', scaled_query, state)
        scaled_key = head_key.astype(jnp.float32) * jnp.exp(block_decay[None, :] - cum_decay)[:, :, None]
        own_state = mix('thd,the->hde', scaled_key, head_value)
        following = jnp.exp(block_decay)[:, None, None] * state + own_state
        return (following, (attention, state))
    initial = jnp.zeros((H, HD, HD), jnp.float32)
    _, (attention, incoming) = lax.scan(forward_step, initial, (query_blocks, key_blocks, value_blocks, decay_blocks))
    normed = head_norm(attention).astype(jnp.bfloat16).reshape(TOKENS, H * HD)
    attn_out = jnp.dot(normed, out_weight, preferred_element_type=jnp.float32).astype(jnp.bfloat16)
    grad_normed = jnp.dot(output_gradient, out_weight.T, preferred_element_type=jnp.float32).reshape(shape)
    _, pullback = jax.vjp(head_norm, attention)
    grad_attention = pullback(grad_normed)[0].astype(jnp.bfloat16)

    def backward_step(carried, inputs):
        head_query, head_key, head_value, decay, state, grad_head = inputs
        cum_decay = jnp.cumsum(decay, axis=0)
        block_decay = cum_decay[-1]
        table = decay_lookup_grid(cum_decay)
        probs = (mix('thd,shd->hts', head_query, head_key) * table).astype(jnp.bfloat16)
        grad_scores = (mix('the,she->hts', grad_head, head_value) * table).astype(jnp.bfloat16)
        rise = jnp.exp(cum_decay)[:, :, None]
        fall = jnp.exp(block_decay[None, :] - cum_decay)[:, :, None]
        scaled_query = head_query.astype(jnp.float32) * rise
        query_gradient_rows = mix('hts,shd->thd', grad_scores, head_key) + rise * mix('the,hde->thd', grad_head, state)
        grad_key = mix('hts,thd->shd', grad_scores, head_query) + fall * mix('the,hde->thd', head_value, carried)
        grad_value = mix('hts,the->she', probs, grad_head) + fall * mix('thd,hde->the', head_key, carried)
        own_grad = mix('thd,the->hde', scaled_query, grad_head)
        following = own_grad + jnp.exp(block_decay)[:, None, None] * carried
        return (following, (query_gradient_rows.astype(jnp.bfloat16), grad_key.astype(jnp.bfloat16), grad_value.astype(jnp.bfloat16)))
    _, (grad_q, grad_k, grad_v) = lax.scan(backward_step, initial, (query_blocks, key_blocks, value_blocks, decay_blocks, incoming, grad_attention), reverse=True)
    return (attn_out, grad_q.reshape(TOKENS, H * HD), grad_k.reshape(TOKENS, H * HD), grad_v.reshape(TOKENS, H * HD))
```

```python
import functools

import jax
import jax.numpy as jnp
from jax import lax
from jax.experimental import pallas as pl
from jax.experimental.pallas import tpu as pltpu
from jax.sharding import PartitionSpec as P

EPS = 1e-05
F32 = jnp.float32
BF16 = jnp.bfloat16
MIB = 1024 * 1024

NN = (((1,), (0,)), ((), ()))
NT = (((1,), (1,)), ((), ()))
TN = (((0,), (0,)), ((), ()))


def dot(left, right, form=NN):
    return lax.dot_general(left, right, form, preferred_element_type=F32)


def call(kernel, grid, in_specs, out_specs, out_shape, scratch=(), flops=0, moved=0, name=None):
    return pl.pallas_call(
        kernel,
        out_shape=out_shape,
        grid_spec=pltpu.PrefetchScalarGridSpec(
            num_scalar_prefetch=1,
            grid=grid,
            in_specs=in_specs,
            out_specs=out_specs,
            scratch_shapes=list(scratch),
        ),
        compiler_params=pltpu.CompilerParams(vmem_limit_bytes=40 * MIB),
        cost_estimate=pl.CostEstimate(flops=flops, bytes_accessed=moved, transcendentals=0),
        name=name,
    )


def whole(shape):
    return pl.BlockSpec(shape, lambda *_: (0,) * len(shape))


def three_terms(x):
    high = x.astype(BF16)
    rest = x - high.astype(F32)
    middle = rest.astype(BF16)
    low = (rest - middle.astype(F32)).astype(BF16)
    return high, middle, low


def column(table, head):
    lane = lax.broadcasted_iota(jnp.int32, table.shape, 1)
    return jnp.sum(jnp.where(lane == head, table, 0.0), axis=1, keepdims=True)


def pack_decays(decays):
    high, middle, low = three_terms(decays)
    rows = [t.astype(F32) for t in (high, middle, low)]
    return jnp.concatenate(rows + [jnp.zeros_like(decays)], axis=0).astype(BF16)


def message_decays(ref):
    rows = ref[512:528, :].astype(F32)
    return rows[0:4] + rows[4:8] + rows[8:12]


def state_kernel(s_ref, ld_ref, km_ref, vm_ref, kp_ref, vp_ref, cum_ref, cumt_ref, mine_ref, send_ref):
    j = pl.program_id(0)
    core = s_ref[0]

    @pl.when(j == 0)
    def _():
        rows = lax.broadcasted_iota(jnp.int32, (512, 512), 0)
        cols = lax.broadcasted_iota(jnp.int32, (512, 512), 1)
        tri = jnp.where(rows >= cols, 1.0, 0.0).astype(BF16)
        total = jnp.zeros((512, 8), F32)
        total_t = jnp.zeros((8, 512), F32)
        for term in three_terms(ld_ref[...])[::-1]:
            total = total + dot(tri, term)
            total_t = total_t + lax.dot_general(
                term, tri, (((0,), (1,)), ((), ())), preferred_element_type=F32
            )
        cum_ref[...] = total
        cumt_ref[...] = total_t

    cum = cum_ref[...]
    for group, k_ref, v_ref, out_ref in ((core, km_ref, vm_ref, mine_ref), (1 - core, kp_ref, vp_ref, send_ref)):
        along = column(cum, group * 4 + j)
        last = along[511:512, :]
        faded = (k_ref[...].astype(F32) * jnp.exp(last - along)).astype(BF16)
        out_ref[pl.ds(pl.multiple_of(j * 128, 128), 128), :] = dot(faded, v_ref[...], TN).astype(BF16)

        @pl.when(j == 0)
        def _():
            decays = jnp.concatenate(
                [jnp.broadcast_to(column(cum[504:512, :], group * 4 + i)[7:8, :], (1, 128)) for i in range(4)],
                axis=0,
            )
            out_ref[512:528, :] = pack_decays(decays)


def own_states(scalars, logdecay, keys, values):
    mine = pl.BlockSpec((512, 128), lambda j, s: (0, s[0] * 4 + j))
    other = pl.BlockSpec((512, 128), lambda j, s: (0, (1 - s[0]) * 4 + j))
    return call(
        state_kernel,
        (4,),
        [whole((512, 8)), mine, mine, other, other],
        [whole((512, 8)), whole((8, 512)), whole((528, 128)), whole((528, 128))],
        [
            jax.ShapeDtypeStruct((512, 8), F32),
            jax.ShapeDtypeStruct((8, 512), F32),
            jax.ShapeDtypeStruct((528, 128), BF16),
            jax.ShapeDtypeStruct((528, 128), BF16),
        ],
        flops=2 * 8 * 512 * 128 * 128,
        moved=3 * MIB,
        name="own_states",
    )(scalars, logdecay, keys, values, keys, values)


def chip_kernel(s_ref, mine_ref, got_ref, out_ref):
    first = s_ref[0] == 0
    d_mine, d_got = message_decays(mine_ref), message_decays(got_ref)
    w_mine = jnp.where(first, jnp.exp(d_got), 1.0)
    w_got = jnp.where(first, 1.0, jnp.exp(d_mine))
    for i in range(4):
        rows = slice(i * 128, i * 128 + 128)
        out_ref[rows, :] = (
            w_mine[i : i + 1] * mine_ref[rows, :].astype(F32) + w_got[i : i + 1] * got_ref[rows, :].astype(F32)
        ).astype(BF16)
    out_ref[512:528, :] = pack_decays(d_mine + d_got)


def chip_total(scalars, mine, got):
    return call(
        chip_kernel,
        (1,),
        [whole((528, 128))] * 2,
        whole((528, 128)),
        jax.ShapeDtypeStruct((528, 128), BF16),
        flops=MIB,
        moved=400 * 1024,
        name="chip_total",
    )(scalars, mine, got)


def prefix_weights(place, decays):
    weights, between = [], jnp.zeros_like(decays[0])
    before = jnp.zeros_like(decays[0])
    for k in range(1, 4):
        weights.append(jnp.where(place >= k, jnp.exp(between), 0.0))
        between = between + decays[k]
        before = before + jnp.where(place >= k, decays[k], 0.0)
    return weights, before


def row_kernel(s_ref, m0, m1, m2, m3, total_ref, prefix_ref, before_ref):
    place = s_ref[1]
    refs = (m0, m1, m2, m3)
    decays = [message_decays(r) for r in refs]
    weights, before = prefix_weights(place, decays)
    places = [lax.rem(place - k + 4, 4) for k in range(4)]
    totals = []
    for k in range(4):
        after = jnp.zeros_like(before)
        for m in range(4):
            if m != k:
                after = after + jnp.where(places[m] > places[k], decays[m], 0.0)
        totals.append(jnp.exp(after))
    for i in range(4):
        rows = slice(i * 128, i * 128 + 128)
        values = [r[rows, :].astype(F32) for r in refs]
        prefix_ref[rows, :] = sum(weights[k - 1][i : i + 1] * values[k] for k in range(1, 4))
        total_ref[rows, :] = sum(totals[k][i : i + 1] * values[k] for k in range(4)).astype(BF16)
    total_ref[512:528, :] = pack_decays(decays[0] + decays[1] + decays[2] + decays[3])
    before_ref[...] = jnp.concatenate([before, before], axis=0)


def row_total(scalars, messages):
    return call(
        row_kernel,
        (1,),
        [whole((528, 128))] * 4,
        [whole((528, 128)), whole((512, 128)), whole((8, 128))],
        [
            jax.ShapeDtypeStruct((528, 128), BF16),
            jax.ShapeDtypeStruct((512, 128), F32),
            jax.ShapeDtypeStruct((8, 128), F32),
        ],
        flops=MIB,
        moved=900 * 1024,
        name="row_total",
    )(scalars, *messages)


def arrive_kernel(s_ref, m1, m2, m3, prefix_ref, before_ref, mine_ref, got_ref, keep_ref, send_ref):
    place = s_ref[2]
    first = s_ref[0] == 0
    refs = (None, m1, m2, m3)
    decays = [None] + [message_decays(r) for r in refs[1:]]
    decays[0] = jnp.zeros_like(decays[1])
    weights, _ = prefix_weights(place, decays)
    fade = jnp.exp(before_ref[0:4, :])
    d_first = jnp.where(first, message_decays(mine_ref), message_decays(got_ref))
    w_first = jnp.exp(d_first)
    for i in range(4):
        rows = slice(i * 128, i * 128 + 128)
        earlier = sum(weights[k - 1][i : i + 1] * refs[k][rows, :].astype(F32) for k in range(1, 4))
        at_first = fade[i : i + 1] * earlier + prefix_ref[rows, :]
        state_first = jnp.where(first, mine_ref[rows, :].astype(F32), got_ref[rows, :].astype(F32))
        at_second = w_first[i : i + 1] * at_first + state_first
        keep_ref[rows, :] = jnp.where(first, at_first, at_second).astype(BF16)
        send_ref[rows, :] = jnp.where(first, at_second, at_first).astype(BF16)


def arrive(scalars, messages, prefix, before, mine, got):
    return call(
        arrive_kernel,
        (1,),
        [whole((528, 128))] * 3 + [whole((512, 128)), whole((8, 128)), whole((528, 128)), whole((528, 128))],
        [whole((512, 128))] * 2,
        [jax.ShapeDtypeStruct((512, 128), BF16)] * 2,
        flops=MIB,
        moved=1100 * 1024,
        name="arrive",
    )(scalars, *messages, prefix, before, mine, got)


SWAP = [(i, i ^ 1) for i in range(32)]


def shifts_x(k):
    return [(i, i // 8 * 8 + (i // 2 + k) % 4 * 2 + i % 2) for i in range(32)]


def shifts_z(k):
    return [(i, i + 8 * k) for i in range(32) if 0 <= i + 8 * k < 32]


def scan_blocks(scalars, mine, send, sign):
    got = lax.ppermute(send, "seq", SWAP)
    chip = chip_total(scalars, mine, got)
    row = [chip] + [lax.ppermute(chip, "seq", shifts_x(sign * k)) for k in (1, 2, 3)]
    total, prefix, before = row_total(scalars, row)
    planes = [lax.ppermute(total, "seq", shifts_z(sign * k)) for k in (1, 2, 3)]
    keep, send_back = arrive(scalars, planes, prefix, before, mine, got)
    return keep, lax.ppermute(send_back, "seq", SWAP)


def decay_block(along, along_t, low, high, cols):
    diff = along[low:high, :] - along_t[:, :cols]
    rows_at = lax.broadcasted_iota(jnp.int32, diff.shape, 0) + low
    cols_at = lax.broadcasted_iota(jnp.int32, diff.shape, 1)
    return jnp.exp(jnp.where(rows_at >= cols_at, diff, -1e30))


def head_of(s_ref):
    return lax.rem(pl.program_id(0) + 4 * s_ref[0], 8)


def forward_kernel(s_ref, cum_ref, cumt_ref, q_ref, k_ref, v_ref, keep_ref, got_ref, normed_ref, att_ref):
    head = head_of(s_ref)
    along = column(cum_ref[...], head)
    along_t = cumt_ref[pl.ds(head, 1), :]
    incoming = jnp.where(pl.program_id(0) < 4, keep_ref[...], got_ref[...])
    for low in (0, 256):
        high = low + 256
        q = q_ref[low:high, :]
        table = decay_block(along, along_t, low, high, high)
        probs = (dot(q, k_ref[:high, :], NT) * table).astype(BF16)
        att = dot(probs, v_ref[:high, :]) + jnp.exp(along[low:high, :]) * dot(q, incoming)
        att_ref[low:high, :] = att
        scale = lax.rsqrt(jnp.mean(att * att, axis=1, keepdims=True) + EPS)
        normed_ref[low:high, :] = (att * scale).astype(BF16)


def head_spec(rows=512):
    return pl.BlockSpec((rows, 128), lambda i, s: (0, lax.rem(i + 4 * s[0], 8)))


def state_specs():
    return [
        pl.BlockSpec((128, 128), lambda i, s: (jnp.minimum(i, 3), 0)),
        pl.BlockSpec((128, 128), lambda i, s: (jnp.maximum(i - 4, 0), 0)),
    ]


def forward(scalars, cum, cum_t, q, k, v, keep, got):
    return call(
        forward_kernel,
        (8,),
        [whole((512, 8)), whole((8, 512))] + [head_spec()] * 3 + state_specs(),
        [head_spec()] * 2,
        [jax.ShapeDtypeStruct((512, 1024), BF16), jax.ShapeDtypeStruct((512, 1024), F32)],
        flops=8 * 6 * 512 * 512 * 128,
        moved=6 * MIB,
        name="forward",
    )(scalars, cum, cum_t, q, k, v, keep, got)


def project_kernel(s_ref, x_ref, w_ref, *refs):
    out_ref = refs[-1]
    total = dot(x_ref[...], w_ref[...])
    for r in refs[:-1]:
        total = total + r[...].astype(F32)
    out_ref[...] = total.astype(BF16)


def project(scalars, slot, normed, half, weight, adds=()):
    rows = 512 if half is None else 256
    start = half or 0
    tile = 512
    part = pl.BlockSpec((rows, tile), lambda n, s: (0, n))
    return call(
        project_kernel,
        (1536 // tile,),
        [
            pl.BlockSpec((rows, 1024), lambda n, s: (start, 0)),
            pl.BlockSpec((1024, tile), lambda n, s: (0, s[slot] * (1536 // tile) + n)),
        ]
        + [part] * len(adds),
        part,
        jax.ShapeDtypeStruct((rows, 1536), BF16),
        flops=2 * rows * 1024 * 1536,
        moved=5 * MIB,
        name="project",
    )(scalars, normed, weight, *adds)


def grad_own_kernel(s_ref, x_ref, w_ref, out_ref):
    out_ref[...] = dot(x_ref[...], w_ref[...], NT)


def grad_own(scalars, x, weight):
    return call(
        grad_own_kernel,
        (4,),
        [whole((512, 1536)), pl.BlockSpec((256, 1536), lambda n, s: (n, s[3]))],
        pl.BlockSpec((512, 256), lambda n, s: (0, n)),
        jax.ShapeDtypeStruct((512, 1024), F32),
        flops=2 * 512 * 1024 * 1536,
        moved=7 * MIB,
        name="grad_own",
    )(scalars, x, weight)


def grad_near_kernel(s_ref, alo, ahi, blo, bhi, wa_ref, wb_ref, acc_ref, out_ref):
    wa, wb = wa_ref[...], wb_ref[...]
    out_ref[:256, :] = acc_ref[:256, :] + dot(alo[...], wa, NT) + dot(blo[...], wb, NT)
    out_ref[256:, :] = acc_ref[256:, :] + dot(ahi[...], wa, NT) + dot(bhi[...], wb, NT)


def grad_near(scalars, pieces, weight, acc):
    tile = pl.BlockSpec((512, 256), lambda n, s: (0, n))
    return call(
        grad_near_kernel,
        (4,),
        [whole((256, 1536))] * 4
        + [
            pl.BlockSpec((256, 1536), lambda n, s: (n, s[4])),
            pl.BlockSpec((256, 1536), lambda n, s: (n, s[5])),
            tile,
        ],
        tile,
        jax.ShapeDtypeStruct((512, 1024), F32),
        flops=4 * 512 * 1024 * 1536,
        moved=12 * MIB,
        name="grad_near",
    )(scalars, *pieces, weight, weight, acc)


def grad_far_kernel(s_ref, c_ref, d_ref, w_ref, acc_ref, att_ref, q_ref, cum_ref, grad_ref, mine_ref, send_ref):
    n = pl.program_id(0)
    w = w_ref[...]
    core = s_ref[6]
    acc = jnp.concatenate([acc_ref[:256, :] + dot(c_ref[...], w, NT), acc_ref[256:, :] + dot(d_ref[...], w, NT)], axis=0)
    cum = cum_ref[...]
    for i in range(2):
        cols = slice(i * 128, i * 128 + 128)
        head = n * 2 + i
        att, grad = att_ref[:, cols], acc[:, cols]
        scale = lax.rsqrt(jnp.mean(att * att, axis=1, keepdims=True) + EPS)
        unit = att * scale
        out = (scale * (grad - unit * jnp.mean(grad * unit, axis=1, keepdims=True))).astype(BF16)
        grad_ref[:, cols] = out
        along = column(cum, head)
        scaled = (q_ref[:, cols].astype(F32) * jnp.exp(along)).astype(BF16)
        state = dot(scaled, out, TN).astype(BF16)
        decay = pl.ds(pl.multiple_of(lax.rem(head, 4) * 128, 128), 128)
        here = lax.div(head, 4) == core

        @pl.when(here)
        def _():
            mine_ref[decay, :] = state

        @pl.when(jnp.logical_not(here))
        def _():
            send_ref[decay, :] = state

    @pl.when(n == 0)
    def _():
        for group, out_ref in ((core, mine_ref), (1 - core, send_ref)):
            decays = jnp.concatenate(
                [jnp.broadcast_to(column(cum[504:512, :], group * 4 + i)[7:8, :], (1, 128)) for i in range(4)],
                axis=0,
            )
            out_ref[512:528, :] = pack_decays(decays)


def grad_far(scalars, c, d, weight, acc, att, q, cum):
    tile = pl.BlockSpec((512, 256), lambda n, s: (0, n))
    return call(
        grad_far_kernel,
        (4,),
        [whole((256, 1536))] * 2
        + [pl.BlockSpec((256, 1536), lambda n, s: (n, s[7])), tile, tile, tile, whole((512, 8))],
        [tile, whole((528, 128)), whole((528, 128))],
        [
            jax.ShapeDtypeStruct((512, 1024), BF16),
            jax.ShapeDtypeStruct((528, 128), BF16),
            jax.ShapeDtypeStruct((528, 128), BF16),
        ],
        flops=2 * 512 * 1024 * 1536,
        moved=11 * MIB,
        name="grad_far",
    )(scalars, c, d, weight, acc, att, q, cum)


def inside_kernel(s_ref, cum_ref, cumt_ref, q_ref, k_ref, v_ref, g_ref, keep_ref, got_ref, gq_ref, gk_ref, gv_ref):
    head = head_of(s_ref)
    along = column(cum_ref[...], head)
    along_t = cumt_ref[pl.ds(head, 1), :]
    incoming = jnp.where(pl.program_id(0) < 4, keep_ref[...], got_ref[...])
    gk, gv = [None, None], [None, None]
    for low in (0, 256):
        high = low + 256
        q, g = q_ref[low:high, :], g_ref[low:high, :]
        k, v = k_ref[:high, :], v_ref[:high, :]
        table = decay_block(along, along_t, low, high, high)
        probs = (dot(q, k, NT) * table).astype(BF16)
        scores = (dot(g, v, NT) * table).astype(BF16)
        gq = dot(scores, k) + jnp.exp(along[low:high, :]) * dot(g, incoming, NT)
        gq_ref[low:high, :] = gq.astype(BF16)
        if low == 0:
            gk[0], gv[0] = dot(scores, q, TN), dot(probs, g, TN)
        else:
            more_k, more_v = dot(scores, q, TN), dot(probs, g, TN)
            gk_ref[:256, :] = gk[0] + more_k[:256]
            gk_ref[256:, :] = more_k[256:]
            gv_ref[:256, :] = gv[0] + more_v[:256]
            gv_ref[256:, :] = more_v[256:]


def inside(scalars, cum, cum_t, q, k, v, grad, keep, got):
    return call(
        inside_kernel,
        (8,),
        [whole((512, 8)), whole((8, 512))] + [head_spec()] * 4 + state_specs(),
        [head_spec()] * 3,
        [
            jax.ShapeDtypeStruct((512, 1024), BF16),
            jax.ShapeDtypeStruct((512, 1024), F32),
            jax.ShapeDtypeStruct((512, 1024), F32),
        ],
        flops=8 * 12 * 512 * 512 * 128,
        moved=10 * MIB,
        name="inside",
    )(scalars, cum, cum_t, q, k, v, grad, keep, got)


def finish_kernel(s_ref, cum_ref, k_ref, v_ref, gk_ref, gv_ref, keep_ref, got_ref, gk_out, gv_out):
    along = column(cum_ref[...], head_of(s_ref))
    fall = jnp.exp(along[511:512, :] - along)
    outgoing = jnp.where(pl.program_id(0) < 4, keep_ref[...], got_ref[...])
    gk_out[...] = (gk_ref[...] + fall * dot(v_ref[...], outgoing, NT)).astype(BF16)
    gv_out[...] = (gv_ref[...] + fall * dot(k_ref[...], outgoing)).astype(BF16)


def finish(scalars, cum, k, v, gk, gv, keep, got):
    return call(
        finish_kernel,
        (8,),
        [whole((512, 8))] + [head_spec()] * 4 + state_specs(),
        [head_spec()] * 2,
        [jax.ShapeDtypeStruct((512, 1024), BF16)] * 2,
        flops=8 * 4 * 512 * 128 * 128,
        moved=8 * MIB,
        name="finish",
    )(scalars, cum, k, v, gk, gv, keep, got)


RIGHT = [(i, (i + 1) % 4) for i in range(4)]
LEFT = [(i, (i + 3) % 4) for i in range(4)]


def body(queries, keys, values, logdecay, out_weight, output_gradient):
    at = lax.axis_index("seq").astype(jnp.int32)
    h = lax.axis_index("head").astype(jnp.int32)
    core, x, z = at % 2, at // 2 % 4, at // 8
    blocks = [h, (h + 3) % 4, (h + 1) % 4]
    scalars = jnp.stack([core, x, z] + blocks + [core, (h + 2) % 4]).astype(jnp.int32)
    back = jnp.stack([1 - core, 3 - x, 3 - z] + blocks + [core, (h + 2) % 4]).astype(jnp.int32)

    right = lambda a: lax.ppermute(a, "head", RIGHT)
    left = lambda a: lax.ppermute(a, "head", LEFT)

    lo, hi = output_gradient[:256], output_gradient[256:]
    a_lo, b_hi = right(lo), left(hi)
    a_hi, b_lo = right(hi), left(lo)
    c_lo, d_hi = right(a_lo), left(b_hi)

    cum, cum_t, mine, send = own_states(scalars, logdecay, keys, values)
    acc = grad_own(scalars, output_gradient, out_weight)
    keep, got = scan_blocks(scalars, mine, send, 1)
    normed, att = forward(scalars, cum, cum_t, queries, keys, values, keep, got)

    acc = grad_near(scalars, (a_lo, a_hi, b_lo, b_hi), out_weight, acc)
    grad, mine_g, send_g = grad_far(scalars, c_lo, d_hi, out_weight, acc, att, queries, cum)
    keep_g, got_g = scan_blocks(back, mine_g, send_g, -1)
    gq, gk, gv = inside(scalars, cum, cum_t, queries, keys, values, grad, keep, got)
    gk, gv = finish(scalars, cum, keys, values, gk, gv, keep_g, got_g)

    from_left = right(project(scalars, 7, normed, 0, out_weight))
    from_right = left(project(scalars, 7, normed, 1, out_weight))
    direct_r = right(project(scalars, 5, normed, 1, out_weight))
    direct_l = left(project(scalars, 4, normed, 0, out_weight))
    joined_r = right(project(scalars, 5, normed, 0, out_weight, (from_left,)))
    joined_l = left(project(scalars, 4, normed, 1, out_weight, (from_right,)))
    top = project(scalars, 3, normed, 0, out_weight, (joined_r, direct_l))
    bottom = project(scalars, 3, normed, 1, out_weight, (direct_r, joined_l))
    return jnp.concatenate([top, bottom], axis=0), gq, gk, gv


def solution(mesh):
    return jax.shard_map(
        body,
        mesh=mesh,
        in_specs=(
            P("seq", "head"),
            P("seq", "head"),
            P("seq", "head"),
            P("seq", "head"),
            P("head", None),
            P("seq", "head"),
        ),
        out_specs=(P("seq", "head"), P("seq", "head"), P("seq", "head"), P("seq", "head")),
        check_vma=False,
    )
```

```python
import functools

import jax
import jax.numpy as jnp
from jax import lax
from jax.experimental import pallas as pl
from jax.experimental.pallas import tpu as pltpu
from jax.sharding import PartitionSpec as P

EPS = 1e-05
F32 = jnp.float32
BF16 = jnp.bfloat16
MIB = 1024 * 1024

NN = (((1,), (0,)), ((), ()))
NT = (((1,), (1,)), ((), ()))
TN = (((0,), (0,)), ((), ()))


def dot(left, right, form=NN):
    return lax.dot_general(left, right, form, preferred_element_type=F32)


VMEM = pl.BlockSpec(memory_space=pltpu.VMEM)
SMEM = pl.BlockSpec(memory_space=pltpu.SMEM)
ANY = pl.BlockSpec(memory_space=pl.ANY)


def call(kernel, name, scalars, args, outs, after=(), flops=0):
    count, waits = len(args), len(after)

    def run(*refs):
        kernel(*refs[: 1 + count], *refs[1 + count + waits :])

    return pl.pallas_call(
        run,
        out_shape=[jax.ShapeDtypeStruct(shape, dtype) for shape, dtype in outs],
        in_specs=[SMEM] + [VMEM] * count + [ANY] * waits,
        out_specs=[VMEM] * len(outs),
        compiler_params=pltpu.CompilerParams(vmem_limit_bytes=12 * MIB),
        cost_estimate=pl.CostEstimate(flops=flops, bytes_accessed=0, transcendentals=0),
        name=name,
    )(scalars, *args, *after)


def three_terms(x):
    high = x.astype(BF16)
    rest = x - high.astype(F32)
    middle = rest.astype(BF16)
    low = (rest - middle.astype(F32)).astype(BF16)
    return high, middle, low


def head_columns(head):
    return slice(head * 128, head * 128 + 128)


def pack_decays(decays):
    high, middle, low = three_terms(decays)
    rows = [t.astype(F32) for t in (high, middle, low)]
    return jnp.concatenate(rows + [jnp.zeros_like(decays)], axis=0).astype(BF16)


def message_decays(ref):
    rows = ref[512:528, :].astype(F32)
    return rows[0:4] + rows[4:8] + rows[8:12]


MESSAGE = ((528, 128), BF16)
STATES = ((512, 128), BF16)


def put_state(core, head, state, mine_ref, send_ref):
    rows = slice(head % 4 * 128, head % 4 * 128 + 128)
    here = core == head // 4

    @pl.when(here)
    def _():
        mine_ref[rows, :] = state

    @pl.when(jnp.logical_not(here))
    def _():
        send_ref[rows, :] = state


def put_decays(core, cum_t, mine_ref, send_ref):
    last = jnp.broadcast_to(cum_t[:, 511:512], (8, 128))
    swap = core == 1
    mine_ref[512:528, :] = pack_decays(jnp.where(swap, last[4:8], last[0:4]))
    send_ref[512:528, :] = pack_decays(jnp.where(swap, last[0:4], last[4:8]))


def state_kernel(s_ref, ld_ref, k_ref, v_ref, cum_ref, cumt_ref, mine_ref, send_ref):
    core = s_ref[6]
    rows = lax.broadcasted_iota(jnp.int32, (512, 512), 0)
    cols = lax.broadcasted_iota(jnp.int32, (512, 512), 1)
    upper = jnp.where(rows <= cols, 1.0, 0.0).astype(BF16)
    lower = jnp.where(rows >= cols, 1.0, 0.0).astype(BF16)
    cum = jnp.zeros((512, 8), F32)
    cum_t = jnp.zeros((8, 512), F32)
    for term in three_terms(ld_ref[...])[::-1]:
        cum = cum + dot(lower, term, NT)
        cum_t = cum_t + dot(term, upper)
    cum_ref[...] = cum
    cumt_ref[...] = cum_t
    fall = jnp.exp(cum[511:512, :] - cum)
    for head in range(8):
        at = head_columns(head)
        faded = (k_ref[:, at].astype(F32) * fall[:, head : head + 1]).astype(BF16)
        put_state(core, head, dot(faded, v_ref[:, at], TN).astype(BF16), mine_ref, send_ref)
    put_decays(core, cum_t, mine_ref, send_ref)


def own_states(scalars, logdecay_t, keys, values):
    return call(
        state_kernel,
        "own_states",
        scalars,
        (logdecay_t, keys, values),
        [((512, 8), F32), ((8, 512), F32), MESSAGE, MESSAGE],
    )


def chip_kernel(base, s_ref, mine_ref, got_ref, out_ref):
    first = s_ref[base] == 0
    d_mine, d_got = message_decays(mine_ref), message_decays(got_ref)
    w_mine = jnp.where(first, jnp.exp(d_got), 1.0)
    w_got = jnp.where(first, 1.0, jnp.exp(d_mine))
    for i in range(4):
        rows = slice(i * 128, i * 128 + 128)
        out_ref[rows, :] = (
            w_mine[i : i + 1] * mine_ref[rows, :].astype(F32) + w_got[i : i + 1] * got_ref[rows, :].astype(F32)
        ).astype(BF16)
    out_ref[512:528, :] = pack_decays(d_mine + d_got)


def prefix_weights(place, decays):
    weights, between = [], jnp.zeros_like(decays[0])
    before = jnp.zeros_like(decays[0])
    for k in range(1, 4):
        weights.append(jnp.where(place >= k, jnp.exp(between), 0.0))
        between = between + decays[k]
        before = before + jnp.where(place >= k, decays[k], 0.0)
    return weights, before


def row_kernel(base, s_ref, m0, m1, m2, m3, total_ref, prefix_ref, before_ref):
    place = s_ref[base + 1]
    refs = (m0, m1, m2, m3)
    decays = [message_decays(r) for r in refs]
    weights, before = prefix_weights(place, decays)
    places = [lax.rem(place - k + 4, 4) for k in range(4)]
    totals = []
    for k in range(4):
        after = jnp.zeros_like(before)
        for m in range(4):
            if m != k:
                after = after + jnp.where(places[m] > places[k], decays[m], 0.0)
        totals.append(jnp.exp(after))
    for i in range(4):
        rows = slice(i * 128, i * 128 + 128)
        values = [r[rows, :].astype(F32) for r in refs]
        prefix_ref[rows, :] = sum(weights[k - 1][i : i + 1] * values[k] for k in range(1, 4))
        total_ref[rows, :] = sum(totals[k][i : i + 1] * values[k] for k in range(4)).astype(BF16)
    total_ref[512:528, :] = pack_decays(decays[0] + decays[1] + decays[2] + decays[3])
    before_ref[...] = jnp.concatenate([before, before], axis=0)


def arrive_kernel(base, s_ref, m1, m2, m3, prefix_ref, before_ref, mine_ref, got_ref, keep_ref, send_ref):
    place = s_ref[base + 2]
    first = s_ref[base] == 0
    refs = (None, m1, m2, m3)
    decays = [None] + [message_decays(r) for r in refs[1:]]
    decays[0] = jnp.zeros_like(decays[1])
    weights, _ = prefix_weights(place, decays)
    fade = jnp.exp(before_ref[0:4, :])
    d_first = jnp.where(first, message_decays(mine_ref), message_decays(got_ref))
    w_first = jnp.exp(d_first)
    for i in range(4):
        rows = slice(i * 128, i * 128 + 128)
        earlier = sum(weights[k - 1][i : i + 1] * refs[k][rows, :].astype(F32) for k in range(1, 4))
        at_first = fade[i : i + 1] * earlier + prefix_ref[rows, :]
        state_first = jnp.where(first, mine_ref[rows, :].astype(F32), got_ref[rows, :].astype(F32))
        at_second = w_first[i : i + 1] * at_first + state_first
        keep_ref[rows, :] = jnp.where(first, at_first, at_second).astype(BF16)
        send_ref[rows, :] = jnp.where(first, at_second, at_first).astype(BF16)


SWAP = [(i, i ^ 1) for i in range(32)]


def shifts_x(k):
    return [(i, i // 8 * 8 + (i // 2 + k) % 4 * 2 + i % 2) for i in range(32)]


def shifts_z(k):
    return [(i, i + 8 * k) for i in range(32) if 0 <= i + 8 * k < 32]


def scan_blocks(scalars, mine, send, sign, beside):
    base = 0 if sign > 0 else 8
    got = lax.ppermute(send, "seq", SWAP)
    (chip,) = call(functools.partial(chip_kernel, base), "chip_total", scalars, (mine, got), [MESSAGE])
    row = [chip] + [lax.ppermute(chip, "seq", shifts_x(sign * k)) for k in (1, 2, 3)]
    first = beside[0]((chip,))
    total, prefix, before = call(
        functools.partial(row_kernel, base),
        "row_total",
        scalars,
        row,
        [MESSAGE, ((512, 128), F32), ((8, 128), F32)],
        first[-1:],
    )
    planes = [lax.ppermute(total, "seq", shifts_z(sign * k)) for k in (1, 2, 3)]
    second = beside[1]((before,), first)
    keep, send_back = call(
        functools.partial(arrive_kernel, base),
        "arrive",
        scalars,
        (*planes, prefix, before, mine, got),
        [STATES, STATES],
        second[-1:],
    )
    return keep, lax.ppermute(send_back, "seq", SWAP), first, second


def decay_block(cum, cum_t, head, low, high):
    diff = cum[low:high, head : head + 1] - cum_t[head : head + 1, :high]
    rows = lax.broadcasted_iota(jnp.int32, diff.shape, 0) + low
    cols = lax.broadcasted_iota(jnp.int32, diff.shape, 1)
    return jnp.exp(jnp.where(rows >= cols, diff, -1e30))


def local_kernel(s_ref, cum_ref, cumt_ref, q_ref, k_ref, v_ref, out_ref):
    cum, cum_t = cum_ref[...], cumt_ref[...]
    for head in range(8):
        at = head_columns(head)
        for low in (0, 256):
            high = low + 256
            table = decay_block(cum, cum_t, head, low, high)
            probs = (dot(q_ref[low:high, at], k_ref[:high, at], NT) * table).astype(BF16)
            out_ref[low:high, at] = dot(probs, v_ref[:high, at])


def local(scalars, cum, cum_t, q, k, v, after):
    return call(local_kernel, "local", scalars, (cum, cum_t, q, k, v), [((512, 1024), F32)], after)


def arrived(s_ref, head, keep_ref, got_ref):
    rows = slice(head % 4 * 128, head % 4 * 128 + 128)
    return jnp.where(s_ref[6] == head // 4, keep_ref[rows, :], got_ref[rows, :])


def attend_kernel(s_ref, local_ref, cum_ref, q_ref, keep_ref, got_ref, normed_ref, att_ref):
    rise = jnp.exp(cum_ref[...])
    for head in range(8):
        at = head_columns(head)
        past = dot(q_ref[:, at], arrived(s_ref, head, keep_ref, got_ref))
        att = local_ref[:, at] + rise[:, head : head + 1] * past
        att_ref[:, at] = att
        scale = lax.rsqrt(jnp.mean(att * att, axis=1, keepdims=True) + EPS)
        normed_ref[:, at] = (att * scale).astype(BF16)


def attend(scalars, local_part, cum, q, keep, got, after):
    return call(
        attend_kernel,
        "attend",
        scalars,
        (local_part, cum, q, keep, got),
        [((512, 1024), BF16), ((512, 1024), F32)],
        after,
    )


HALF = ((256, 1536), BF16)
WIDE_HALF = ((256, 1536), F32)


def block_columns(s_ref, slot, offset=0, size=1536):
    return pl.ds(pl.multiple_of(s_ref[slot] * 1536 + offset, 128), size)


def products(s_ref, x_ref, w_ref, slot, top_ref, bottom_ref):
    for offset in (0, 512, 1024):
        out = dot(x_ref[...], w_ref[:, block_columns(s_ref, slot, offset, 512)])
        at = slice(offset, offset + 512)
        top_ref[:, at] = out[:256].astype(top_ref.dtype)
        bottom_ref[:, at] = out[256:].astype(bottom_ref.dtype)


def project_near_kernel(s_ref, x_ref, w_ref, right_top, right_bottom, left_top, left_bottom):
    products(s_ref, x_ref, w_ref, 5, right_top, right_bottom)
    products(s_ref, x_ref, w_ref, 4, left_top, left_bottom)


def project_one_kernel(slot, s_ref, x_ref, w_ref, top_ref, bottom_ref):
    products(s_ref, x_ref, w_ref, slot, top_ref, bottom_ref)


def split_kernel(s_ref, a_ref, b_ref, top_ref, bottom_ref):
    top_ref[...] = a_ref[:256, :]
    bottom_ref[...] = b_ref[256:, :]


def round_kernel(s_ref, a_ref, b_ref, a_out, b_out):
    a_out[...] = a_ref[...].astype(BF16)
    b_out[...] = b_ref[...].astype(BF16)


def join_kernel(s_ref, right_ref, from_left, left_ref, from_right, out_right, out_left):
    out_right[...] = (right_ref[...] + from_left[...].astype(F32)).astype(BF16)
    out_left[...] = (left_ref[...] + from_right[...].astype(F32)).astype(BF16)


def total_kernel(s_ref, top_ref, bottom_ref, top_a, top_b, bottom_a, bottom_b, out_ref):
    out_ref[:256, :] = (top_ref[...] + top_a[...].astype(F32) + top_b[...].astype(F32)).astype(BF16)
    out_ref[256:, :] = (bottom_ref[...] + bottom_a[...].astype(F32) + bottom_b[...].astype(F32)).astype(BF16)


def grad_own_kernel(s_ref, x_ref, w_ref, out_ref):
    for low in range(0, 1024, 256):
        rows = slice(low, low + 256)
        out_ref[:, rows] = dot(x_ref[...], w_ref[rows, block_columns(s_ref, 3)], NT)


def grad_near_kernel(s_ref, a_ref, b_ref, w_ref, acc_ref, out_ref):
    for low in range(0, 1024, 256):
        rows = slice(low, low + 256)
        out_ref[:, rows] = (
            acc_ref[:, rows]
            + dot(a_ref[...], w_ref[rows, block_columns(s_ref, 4)], NT)
            + dot(b_ref[...], w_ref[rows, block_columns(s_ref, 5)], NT)
        )


def grad_far_kernel(s_ref, c_ref, d_ref, w_ref, acc_ref, att_ref, q_ref, cum_ref, cumt_ref, grad_ref, mine_ref, send_ref):
    core = s_ref[6]
    rise = jnp.exp(cum_ref[...])
    x = jnp.concatenate([c_ref[...], d_ref[...]], axis=0)
    for low in range(0, 1024, 256):
        rows = slice(low, low + 256)
        acc = acc_ref[:, rows] + dot(x, w_ref[rows, block_columns(s_ref, 7)], NT)
        for i in range(2):
            head = low // 128 + i
            at = head_columns(head)
            att, grad = att_ref[:, at], acc[:, i * 128 : i * 128 + 128]
            scale = lax.rsqrt(jnp.mean(att * att, axis=1, keepdims=True) + EPS)
            unit = att * scale
            out = (scale * (grad - unit * jnp.mean(grad * unit, axis=1, keepdims=True))).astype(BF16)
            grad_ref[:, at] = out
            scaled = (q_ref[:, at].astype(F32) * rise[:, head : head + 1]).astype(BF16)
            put_state(core, head, dot(scaled, out, TN).astype(BF16), mine_ref, send_ref)
    put_decays(core, cumt_ref[...], mine_ref, send_ref)


def inside_kernel(heads, s_ref, cum_ref, cumt_ref, q_ref, k_ref, v_ref, g_ref, keep_ref, got_ref, *refs):
    gq_ref, gk_ref, gv_ref = refs[-3:]
    cum, cum_t = cum_ref[...], cumt_ref[...]
    rise = jnp.exp(cum)
    if len(refs) > 3:
        gq_ref[:, :512] = refs[0][...]
    for head in heads:
        at = head_columns(head)
        to = head_columns(head - heads[0])
        to_q = at if len(refs) > 3 else to
        incoming = arrived(s_ref, head, keep_ref, got_ref)
        early_k = early_v = None
        for low in (0, 256):
            high = low + 256
            q, g = q_ref[low:high, at], g_ref[low:high, at]
            k, v = k_ref[:high, at], v_ref[:high, at]
            table = decay_block(cum, cum_t, head, low, high)
            probs = (dot(q, k, NT) * table).astype(BF16)
            scores = (dot(g, v, NT) * table).astype(BF16)
            gq = dot(scores, k) + rise[low:high, head : head + 1] * dot(g, incoming, NT)
            gq_ref[low:high, to_q] = gq.astype(BF16)
            part_k, part_v = dot(scores, q, TN), dot(probs, g, TN)
            if low == 0:
                early_k, early_v = part_k, part_v
            else:
                gk_ref[:256, to] = early_k + part_k[:256]
                gk_ref[256:, to] = part_k[256:]
                gv_ref[:256, to] = early_v + part_v[:256]
                gv_ref[256:, to] = part_v[256:]


def finish_kernel(s_ref, cum_ref, k_ref, v_ref, gk_a, gv_a, gk_b, gv_b, keep_ref, got_ref, gk_out, gv_out):
    cum = cum_ref[...]
    fall = jnp.exp(cum[511:512, :] - cum)
    for head in range(8):
        at, part = head_columns(head), head_columns(head % 4)
        gk_ref, gv_ref = ((gk_a, gv_a), (gk_b, gv_b))[head // 4]
        outgoing = arrived(s_ref, head, keep_ref, got_ref)
        factor = fall[:, head : head + 1]
        gk_out[:, at] = (gk_ref[:, part] + factor * dot(v_ref[:, at], outgoing, NT)).astype(BF16)
        gv_out[:, at] = (gv_ref[:, part] + factor * dot(k_ref[:, at], outgoing)).astype(BF16)


RIGHT = [(i, (i + 1) % 4) for i in range(4)]
LEFT = [(i, (i + 3) % 4) for i in range(4)]


def body(queries, keys, values, logdecay, weight, output_gradient):
    at = lax.axis_index("seq").astype(jnp.int32)
    h = lax.axis_index("head").astype(jnp.int32)
    core, x, z = at % 2, at // 2 % 4, at // 8
    blocks = [h, (h + 3) % 4, (h + 1) % 4]
    scalars = jnp.stack([core, x, z] + blocks + [core, (h + 2) % 4, 1 - core, 3 - x, 3 - z]).astype(jnp.int32)

    right = lambda a: lax.ppermute(a, "head", RIGHT)
    left = lambda a: lax.ppermute(a, "head", LEFT)
    wide, narrow = ((512, 1024), F32), ((512, 1024), BF16)
    wide_part, narrow_part = ((512, 512), F32), ((512, 512), BF16)

    a, b = right(output_gradient), left(output_gradient)

    cum, cum_t, mine, send = own_states(scalars, logdecay.T, keys, values)
    keep, got, (local_part,), (acc,) = scan_blocks(
        scalars,
        mine,
        send,
        1,
        (
            lambda after: local(scalars, cum, cum_t, queries, keys, values, after),
            lambda after, _: call(grad_own_kernel, "grad_own", scalars, (output_gradient, weight), [wide], after),
        ),
    )
    a_top, b_bottom = call(split_kernel, "split", scalars, (a, b), [HALF, HALF], (keep,))
    c, d = right(a_top), left(b_bottom)
    normed, att = attend(scalars, local_part, cum, queries, keep, got, (a_top,))

    (acc,) = call(grad_near_kernel, "grad_near", scalars, (a, b, weight, acc), [wide], (att,))
    near = call(project_near_kernel, "project_near", scalars, (normed, weight), [WIDE_HALF] * 4, (acc,))
    right_top, right_bottom, left_top, left_bottom = near
    own = call(
        functools.partial(project_one_kernel, 3), "project_own", scalars, (normed, weight), [WIDE_HALF] * 2, near[:1]
    )
    far = call(functools.partial(project_one_kernel, 7), "project_far", scalars, (normed, weight), [HALF] * 2, own[:1])
    from_left, from_right = right(far[0]), left(far[1])
    grad, mine_g, send_g = call(
        grad_far_kernel,
        "grad_far",
        scalars,
        (c, d, weight, acc, att, queries, cum, cum_t),
        [narrow, MESSAGE, MESSAGE],
        far[:1],
    )
    inputs = (cum, cum_t, queries, keys, values, grad, keep, got)
    direct, joined = [], []

    def first(after):
        direct.extend(call(round_kernel, "direct", scalars, (right_bottom, left_top), [HALF, HALF], after))
        return call(
            functools.partial(inside_kernel, range(0, 4)),
            "inside_a",
            scalars,
            inputs,
            [narrow_part, wide_part, wide_part],
            direct[:1],
        )

    def second(after, one):
        joined.extend(
            call(join_kernel, "join", scalars, (right_top, from_left, left_bottom, from_right), [HALF, HALF], after)
        )
        return call(
            functools.partial(inside_kernel, range(4, 8)),
            "inside_b",
            scalars,
            inputs + (one[0],),
            [narrow, wide_part, wide_part],
            joined[:1],
        )

    keep_g, got_g, (_, gk_a, gv_a), (gq, gk_b, gv_b) = scan_blocks(scalars, mine_g, send_g, -1, (first, second))
    direct_r, direct_l = right(direct[0]), left(direct[1])
    joined_r, joined_l = right(joined[0]), left(joined[1])
    gk, gv = call(
        finish_kernel,
        "finish",
        scalars,
        (cum, keys, values, gk_a, gv_a, gk_b, gv_b, keep_g, got_g),
        [narrow, narrow],
    )
    (out,) = call(
        total_kernel,
        "total",
        scalars,
        (*own, joined_r, direct_l, direct_r, joined_l),
        [((512, 1536), BF16)],
        (gk,),
    )
    return out, gq, gk, gv


def solution(mesh):
    return jax.shard_map(
        body,
        mesh=mesh,
        in_specs=(
            P("seq", "head"),
            P("seq", "head"),
            P("seq", "head"),
            P("seq", "head"),
            P("head", None),
            P("seq", "head"),
        ),
        out_specs=(P("seq", "head"), P("seq", "head"), P("seq", "head"), P("seq", "head")),
        check_vma=False,
    )
```

```python
import functools

import jax
import jax.numpy as jnp
from jax import lax
from jax.experimental import pallas as pl
from jax.experimental.pallas import tpu as pltpu
from jax.sharding import PartitionSpec as P

EPS = 1e-05
F32 = jnp.float32
BF16 = jnp.bfloat16
MIB = 1024 * 1024
GIGA = 10**9

NN = (((1,), (0,)), ((), ()))
NT = (((1,), (1,)), ((), ()))
TN = (((0,), (0,)), ((), ()))


def dot(left, right, form=NN):
    return lax.dot_general(left, right, form, preferred_element_type=F32)


VMEM = pl.BlockSpec(memory_space=pltpu.VMEM)
SMEM = pl.BlockSpec(memory_space=pltpu.SMEM)
ANY = pl.BlockSpec(memory_space=pl.ANY)
HBM = pl.BlockSpec(memory_space=pltpu.HBM)


COST = dict(
    own_states=4 * GIGA,
    chip_total=GIGA // 2,
    local=5 * GIGA,
    row_total=GIGA // 2,
    grad_own=2 * GIGA,
    arrive=GIGA // 2,
    split=GIGA // 2,
    attend=GIGA,
    grad_near=4 * GIGA,
    project_far=2 * GIGA,
    project_near=4 * GIGA,
    project_own=2 * GIGA,
    grad_far=6 * GIGA,
    join=GIGA,
    inside=8 * GIGA,
    finish=3 * GIGA,
    total=2 * GIGA,
)


def call(kernel, name, scalars, args, outs, after=(), far=(), far_outs=(), scratch=(), room=12):
    count, waits = len(args), len(after)

    def run(*refs):
        kernel(*refs[: 1 + count], *refs[1 + count + waits :])

    return pl.pallas_call(
        run,
        out_shape=[jax.ShapeDtypeStruct(shape, dtype) for shape, dtype in outs],
        in_specs=[SMEM] + [HBM if i in far else VMEM for i in range(count)] + [ANY] * waits,
        out_specs=[HBM if i in far_outs else VMEM for i in range(len(outs))],
        scratch_shapes=list(scratch),
        compiler_params=pltpu.CompilerParams(vmem_limit_bytes=room * MIB),
        cost_estimate=pl.CostEstimate(flops=COST[name], bytes_accessed=0, transcendentals=0),
        name=name,
    )(scalars, *args, *after)


def three_terms(x):
    high = x.astype(BF16)
    rest = x - high.astype(F32)
    middle = rest.astype(BF16)
    low = (rest - middle.astype(F32)).astype(BF16)
    return high, middle, low


def head_columns(head):
    return slice(head * 128, head * 128 + 128)


def pack_decays(decays):
    high, middle, low = three_terms(decays)
    rows = [t.astype(F32) for t in (high, middle, low)]
    return jnp.concatenate(rows + [jnp.zeros_like(decays)], axis=0).astype(BF16)


def message_decays(ref):
    rows = ref[512:528, :].astype(F32)
    return rows[0:4] + rows[4:8] + rows[8:12]


MESSAGE = ((528, 128), BF16)
STATES = ((512, 128), BF16)


def put_state(core, head, state, mine_ref, send_ref):
    rows = slice(head % 4 * 128, head % 4 * 128 + 128)
    here = core == head // 4

    @pl.when(here)
    def _():
        mine_ref[rows, :] = state

    @pl.when(jnp.logical_not(here))
    def _():
        send_ref[rows, :] = state


def put_decays(core, cum_t, mine_ref, send_ref):
    last = jnp.broadcast_to(cum_t[:, 511:512], (8, 128))
    swap = core == 1
    mine_ref[512:528, :] = pack_decays(jnp.where(swap, last[4:8], last[0:4]))
    send_ref[512:528, :] = pack_decays(jnp.where(swap, last[0:4], last[4:8]))


def state_kernel(s_ref, ld_ref, q_hbm, k_hbm, v_hbm, cum_ref, cumt_ref, mine_ref, send_ref, q_ref, k_ref, v_ref, sems):
    core = s_ref[6]
    loads = []
    for part in range(4):
        cols = slice(part * 256, part * 256 + 256)
        pair = [
            pltpu.make_async_copy(far.at[:, cols], near.at[:, cols], sems.at[part * 2 + i])
            for i, (far, near) in enumerate(((k_hbm, k_ref), (v_hbm, v_ref)))
        ]
        for copy in pair:
            copy.start()
        loads.append(pair)
    load_q = pltpu.make_async_copy(q_hbm, q_ref, sems.at[8])
    load_q.start()

    rows = lax.broadcasted_iota(jnp.int32, (512, 512), 0)
    cols = lax.broadcasted_iota(jnp.int32, (512, 512), 1)
    upper = jnp.where(rows <= cols, 1.0, 0.0).astype(BF16)
    lower = jnp.where(rows >= cols, 1.0, 0.0).astype(BF16)
    cum = jnp.zeros((512, 8), F32)
    cum_t = jnp.zeros((8, 512), F32)
    for term in three_terms(ld_ref[...])[::-1]:
        cum = cum + dot(lower, term, NT)
        cum_t = cum_t + dot(term, upper)
    cum_ref[...] = cum
    cumt_ref[...] = cum_t
    fall = jnp.exp(cum[511:512, :] - cum)
    for head in range(8):
        if head % 2 == 0:
            for copy in loads[head // 2]:
                copy.wait()
        at = head_columns(head)
        faded = (k_ref[:, at].astype(F32) * fall[:, head : head + 1]).astype(BF16)
        put_state(core, head, dot(faded, v_ref[:, at], TN).astype(BF16), mine_ref, send_ref)
    put_decays(core, cum_t, mine_ref, send_ref)
    load_q.wait()


def own_states(scalars, logdecay_t, queries, keys, values):
    held = ((512, 1024), BF16)
    return call(
        state_kernel,
        "own_states",
        scalars,
        (logdecay_t, queries, keys, values),
        [((512, 8), F32), ((8, 512), F32), MESSAGE, MESSAGE, held, held, held],
        far=(1, 2, 3),
        scratch=[pltpu.SemaphoreType.DMA((9,))],
        room=50,
    )


def chip_kernel(base, s_ref, mine_ref, got_ref, out_ref):
    first = s_ref[base] == 0
    d_mine, d_got = message_decays(mine_ref), message_decays(got_ref)
    w_mine = jnp.where(first, jnp.exp(d_got), 1.0)
    w_got = jnp.where(first, 1.0, jnp.exp(d_mine))
    for i in range(4):
        rows = slice(i * 128, i * 128 + 128)
        out_ref[rows, :] = (
            w_mine[i : i + 1] * mine_ref[rows, :].astype(F32) + w_got[i : i + 1] * got_ref[rows, :].astype(F32)
        ).astype(BF16)
    out_ref[512:528, :] = pack_decays(d_mine + d_got)


def prefix_weights(place, decays):
    weights, between = [], jnp.zeros_like(decays[0])
    before = jnp.zeros_like(decays[0])
    for k in range(1, 4):
        weights.append(jnp.where(place >= k, jnp.exp(between), 0.0))
        between = between + decays[k]
        before = before + jnp.where(place >= k, decays[k], 0.0)
    return weights, before


def row_kernel(base, s_ref, m0, m1, m2, m3, total_ref, prefix_ref, before_ref):
    place = s_ref[base + 1]
    refs = (m0, m1, m2, m3)
    decays = [message_decays(r) for r in refs]
    weights, before = prefix_weights(place, decays)
    places = [lax.rem(place - k + 4, 4) for k in range(4)]
    totals = []
    for k in range(4):
        after = jnp.zeros_like(before)
        for m in range(4):
            if m != k:
                after = after + jnp.where(places[m] > places[k], decays[m], 0.0)
        totals.append(jnp.exp(after))
    for i in range(4):
        rows = slice(i * 128, i * 128 + 128)
        values = [r[rows, :].astype(F32) for r in refs]
        prefix_ref[rows, :] = sum(weights[k - 1][i : i + 1] * values[k] for k in range(1, 4))
        total_ref[rows, :] = sum(totals[k][i : i + 1] * values[k] for k in range(4)).astype(BF16)
    total_ref[512:528, :] = pack_decays(decays[0] + decays[1] + decays[2] + decays[3])
    before_ref[...] = jnp.concatenate([before, before], axis=0)


def arrive_kernel(base, s_ref, m1, m2, m3, prefix_ref, before_ref, mine_ref, got_ref, keep_ref, send_ref):
    place = s_ref[base + 2]
    first = s_ref[base] == 0
    refs = (None, m1, m2, m3)
    decays = [None] + [message_decays(r) for r in refs[1:]]
    decays[0] = jnp.zeros_like(decays[1])
    weights, _ = prefix_weights(place, decays)
    fade = jnp.exp(before_ref[0:4, :])
    d_first = jnp.where(first, message_decays(mine_ref), message_decays(got_ref))
    w_first = jnp.exp(d_first)
    for i in range(4):
        rows = slice(i * 128, i * 128 + 128)
        earlier = sum(weights[k - 1][i : i + 1] * refs[k][rows, :].astype(F32) for k in range(1, 4))
        at_first = fade[i : i + 1] * earlier + prefix_ref[rows, :]
        state_first = jnp.where(first, mine_ref[rows, :].astype(F32), got_ref[rows, :].astype(F32))
        at_second = w_first[i : i + 1] * at_first + state_first
        keep_ref[rows, :] = jnp.where(first, at_first, at_second).astype(BF16)
        send_ref[rows, :] = jnp.where(first, at_second, at_first).astype(BF16)


SWAP = [(i, i ^ 1) for i in range(32)]


def shifts_x(k):
    return [(i, i // 8 * 8 + (i // 2 + k) % 4 * 2 + i % 2) for i in range(32)]


def shifts_z(k):
    return [(i, i + 8 * k) for i in range(32) if 0 <= i + 8 * k < 32]


def scan_blocks(scalars, mine, send, sign, beside):
    base = 0 if sign > 0 else 8
    got = lax.ppermute(send, "seq", SWAP)
    (chip,) = call(functools.partial(chip_kernel, base), "chip_total", scalars, (mine, got), [MESSAGE])
    row = [chip] + [lax.ppermute(chip, "seq", shifts_x(sign * k)) for k in (1, 2, 3)]
    first = beside[0]((chip,))
    total, prefix, before = call(
        functools.partial(row_kernel, base),
        "row_total",
        scalars,
        row,
        [MESSAGE, ((512, 128), F32), ((8, 128), F32)],
        first[-1:],
    )
    planes = [lax.ppermute(total, "seq", shifts_z(sign * k)) for k in (1, 2, 3)]
    second = beside[1]((before,), first)
    keep, send_back = call(
        functools.partial(arrive_kernel, base),
        "arrive",
        scalars,
        (*planes, prefix, before, mine, got),
        [STATES, STATES],
        second[-1:],
    )
    return keep, lax.ppermute(send_back, "seq", SWAP), first, second


def decay_block(cum, cum_t, head, low, high):
    diff = cum[low:high, head : head + 1] - cum_t[head : head + 1, :high]
    rows = lax.broadcasted_iota(jnp.int32, diff.shape, 0) + low
    cols = lax.broadcasted_iota(jnp.int32, diff.shape, 1)
    return jnp.exp(jnp.where(rows >= cols, diff, -1e30))


def local_kernel(s_ref, cum_ref, cumt_ref, q_ref, k_ref, v_ref, w_hbm, out_ref, scaled_ref, turned_ref, w_ref, sems):
    loads = []
    for part in range(4):
        rows = slice(part * 256, part * 256 + 256)
        loads.append(pltpu.make_async_copy(w_hbm.at[rows, :], w_ref.at[rows, :], sems.at[part]))
        loads[-1].start()
    cum, cum_t = cum_ref[...], cumt_ref[...]
    rise = jnp.exp(cum)
    for head in range(8):
        at = head_columns(head)
        scaled = q_ref[:, at].astype(F32) * rise[:, head : head + 1]
        scaled_ref[:, at] = scaled.astype(BF16)
        turned_ref[at, :] = scaled.T.astype(BF16)
        for low in (0, 256):
            high = low + 256
            table = decay_block(cum, cum_t, head, low, high)
            probs = (dot(q_ref[low:high, at], k_ref[:high, at], NT) * table).astype(BF16)
            out_ref[low:high, at] = dot(probs, v_ref[:high, at])
    for copy in loads:
        copy.wait()


def local(scalars, cum, cum_t, q, k, v, weight, after):
    return call(
        local_kernel,
        "local",
        scalars,
        (cum, cum_t, q, k, v, weight),
        [((512, 1024), F32), ((512, 1024), BF16), ((1024, 512), BF16), ((1024, 6144), BF16)],
        after,
        far=(5,),
        room=34,
        scratch=[pltpu.SemaphoreType.DMA((4,))],
    )


def arrived(s_ref, head, keep_ref, got_ref):
    rows = slice(head % 4 * 128, head % 4 * 128 + 128)
    return jnp.where(s_ref[6] == head // 4, keep_ref[rows, :], got_ref[rows, :])


def attend_kernel(s_ref, local_ref, scaled_ref, keep_ref, got_ref, normed_ref, unit_ref, scale_ref):
    for head in range(8):
        at = head_columns(head)
        att = local_ref[:, at] + dot(scaled_ref[:, at], arrived(s_ref, head, keep_ref, got_ref))
        scale = lax.rsqrt(jnp.mean(att * att, axis=1, keepdims=True) + EPS)
        unit = att * scale
        unit_ref[:, at] = unit
        scale_ref[:, at] = jnp.broadcast_to(scale, unit.shape)
        normed_ref[:, at] = unit.astype(BF16)


HALF = ((256, 1536), BF16)
WHOLE = ((512, 1536), BF16)
WIDE_HALF = ((256, 1536), F32)


def block_columns(s_ref, slot, offset=0, size=1536):
    return pl.ds(pl.multiple_of(s_ref[slot] * 1536 + offset, 128), size)


def products(s_ref, x_ref, w_ref, slot, top_ref, bottom_ref):
    for offset in (0, 512, 1024):
        out = dot(x_ref[...], w_ref[:, block_columns(s_ref, slot, offset, 512)])
        at = slice(offset, offset + 512)
        top_ref[:, at] = out[:256].astype(top_ref.dtype)
        bottom_ref[:, at] = out[256:].astype(bottom_ref.dtype)


def project_near_kernel(s_ref, x_ref, w_ref, right_top, right_bottom, left_top, left_bottom):
    products(s_ref, x_ref, w_ref, 5, right_top, right_bottom)
    products(s_ref, x_ref, w_ref, 4, left_top, left_bottom)


def project_one_kernel(slot, s_ref, x_ref, w_ref, top_ref, bottom_ref):
    products(s_ref, x_ref, w_ref, slot, top_ref, bottom_ref)


def split_kernel(s_ref, a_ref, b_ref, top_ref, bottom_ref):
    top_ref[...] = a_ref[:256, :]
    bottom_ref[...] = b_ref[256:, :]


def join_kernel(s_ref, right_top, right_bottom, left_top, left_bottom, from_left, from_right, out_right, out_left):
    out_right[:256, :] = (right_top[...] + from_left[...].astype(F32)).astype(BF16)
    out_right[256:, :] = right_bottom[...]
    out_left[:256, :] = left_top[...]
    out_left[256:, :] = (left_bottom[...] + from_right[...].astype(F32)).astype(BF16)


def total_kernel(s_ref, top_ref, bottom_ref, a_ref, b_ref, out_ref, out_held, sems):
    copies = []
    for i, own_ref in enumerate((top_ref, bottom_ref)):
        for j in range(2):
            rows = slice(j * 128, j * 128 + 128)
            here = slice(i * 256 + j * 128, i * 256 + j * 128 + 128)
            total = own_ref[rows, :] + a_ref[here, :].astype(F32) + b_ref[here, :].astype(F32)
            out_held[here, :] = total.astype(BF16)
            copies.append(pltpu.make_async_copy(out_held.at[here, :], out_ref.at[here, :], sems.at[i * 2 + j]))
            copies[-1].start()
    for copy in copies:
        copy.wait()


def grad_own_kernel(s_ref, x_ref, w_ref, out_ref):
    for low in range(0, 1024, 256):
        rows = slice(low, low + 256)
        out_ref[:, rows] = dot(x_ref[...], w_ref[rows, block_columns(s_ref, 3)], NT)


def grad_near_kernel(s_ref, a_ref, b_ref, w_ref, acc_ref, out_ref):
    for low in range(0, 1024, 256):
        rows = slice(low, low + 256)
        out_ref[:, rows] = (
            acc_ref[:, rows]
            + dot(a_ref[...], w_ref[rows, block_columns(s_ref, 4)], NT)
            + dot(b_ref[...], w_ref[rows, block_columns(s_ref, 5)], NT)
        )


def grad_far_kernel(
    s_ref, c_ref, d_ref, w_ref, acc_ref, unit_ref, scale_ref, turned_ref, cumt_ref, grad_ref, mine_ref, send_ref
):
    core = s_ref[6]
    x = jnp.concatenate([c_ref[...], d_ref[...]], axis=0)
    for low in range(0, 1024, 256):
        rows = slice(low, low + 256)
        acc = acc_ref[:, rows] + dot(x, w_ref[rows, block_columns(s_ref, 7)], NT)
        for i in range(2):
            head = low // 128 + i
            at = head_columns(head)
            unit, grad = unit_ref[:, at], acc[:, i * 128 : i * 128 + 128]
            along = jnp.mean(grad * unit, axis=1, keepdims=True)
            out = (scale_ref[:, at] * (grad - unit * along)).astype(BF16)
            grad_ref[:, at] = out
            put_state(core, head, dot(turned_ref[at, :], out).astype(BF16), mine_ref, send_ref)
    put_decays(core, cumt_ref[...], mine_ref, send_ref)


def inside_kernel(s_ref, cum_ref, cumt_ref, q_ref, k_ref, v_ref, g_ref, keep_ref, got_ref, gq_ref, gk_ref, gv_ref):
    cum, cum_t = cum_ref[...], cumt_ref[...]
    rise = jnp.exp(cum)
    for head in range(8):
        at = head_columns(head)
        incoming = arrived(s_ref, head, keep_ref, got_ref)
        early_k = early_v = None
        for low in (0, 256):
            high = low + 256
            q, g = q_ref[low:high, at], g_ref[low:high, at]
            k, v = k_ref[:high, at], v_ref[:high, at]
            table = decay_block(cum, cum_t, head, low, high)
            probs = (dot(q, k, NT) * table).astype(BF16)
            scores = (dot(g, v, NT) * table).astype(BF16)
            gq = dot(scores, k) + rise[low:high, head : head + 1] * dot(g, incoming, NT)
            gq_ref[low:high, at] = gq.astype(BF16)
            part_k, part_v = dot(scores, q, TN), dot(probs, g, TN)
            if low == 0:
                early_k, early_v = part_k, part_v
            else:
                gk_ref[:256, at] = early_k + part_k[:256]
                gk_ref[256:, at] = part_k[256:]
                gv_ref[:256, at] = early_v + part_v[:256]
                gv_ref[256:, at] = part_v[256:]


def finish_kernel(
    s_ref, cum_ref, k_ref, v_ref, gk_ref, gv_ref, keep_ref, got_ref, gk_out, gv_out, order_ref, gk_held, gv_held, sems
):
    cum = cum_ref[...]
    fall = jnp.exp(cum[511:512, :] - cum)
    copies = []
    for head in range(8):
        at = head_columns(head)
        outgoing = arrived(s_ref, head, keep_ref, got_ref)
        factor = fall[:, head : head + 1]
        gk_held[:, at] = (gk_ref[:, at] + factor * dot(v_ref[:, at], outgoing, NT)).astype(BF16)
        gv_held[:, at] = (gv_ref[:, at] + factor * dot(k_ref[:, at], outgoing)).astype(BF16)
        if head % 2 == 1:
            done = slice(head * 128 - 128, head * 128 + 128)
            for i, (held, out) in enumerate(((gk_held, gk_out), (gv_held, gv_out))):
                copies.append(pltpu.make_async_copy(held.at[:, done], out.at[:, done], sems.at[head - 1 + i]))
                copies[-1].start()
    order_ref[...] = jnp.zeros((8, 128), F32)
    for copy in copies:
        copy.wait()


RIGHT = [(i, (i + 1) % 4) for i in range(4)]
LEFT = [(i, (i + 3) % 4) for i in range(4)]


def body(queries, keys, values, logdecay, weight, output_gradient):
    at = lax.axis_index("seq").astype(jnp.int32)
    h = lax.axis_index("head").astype(jnp.int32)
    core, x, z = at % 2, at // 2 % 4, at // 8
    blocks = [h, (h + 3) % 4, (h + 1) % 4]
    scalars = jnp.stack([core, x, z] + blocks + [core, (h + 2) % 4, 1 - core, 3 - x, 3 - z]).astype(jnp.int32)

    right = lambda a: lax.ppermute(a, "head", RIGHT)
    left = lambda a: lax.ppermute(a, "head", LEFT)
    wide, narrow = ((512, 1024), F32), ((512, 1024), BF16)

    a, b = right(output_gradient), left(output_gradient)

    cum, cum_t, mine, send, q, k, v = own_states(scalars, logdecay.T, queries, keys, values)
    keep, got, (local_part, scaled, turned, w), (acc,) = scan_blocks(
        scalars,
        mine,
        send,
        1,
        (
            lambda after: local(scalars, cum, cum_t, q, k, v, weight, after),
            lambda after, one: call(grad_own_kernel, "grad_own", scalars, (output_gradient, one[3]), [wide], after),
        ),
    )
    a_top, b_bottom = call(
        split_kernel,
        "split",
        scalars,
        (a, b),
        [HALF, HALF],
        (keep,),
    )
    c, d = right(a_top), left(b_bottom)
    normed, unit, scale = call(
        attend_kernel, "attend", scalars, (local_part, scaled, keep, got), [narrow, wide, wide], (a_top,)
    )

    (acc,) = call(grad_near_kernel, "grad_near", scalars, (a, b, w, acc), [wide], (unit,))
    far = call(functools.partial(project_one_kernel, 7), "project_far", scalars, (normed, w), [HALF] * 2, (acc,))
    from_left, from_right = right(far[0]), left(far[1])
    near = call(
        project_near_kernel, "project_near", scalars, (normed, w), [WIDE_HALF, HALF, HALF, WIDE_HALF], far[:1]
    )
    own = call(functools.partial(project_one_kernel, 3), "project_own", scalars, (normed, w), [WIDE_HALF] * 2, near[:1])
    grad, mine_g, send_g = call(
        grad_far_kernel,
        "grad_far",
        scalars,
        (c, d, w, acc, unit, scale, turned, cum_t),
        [narrow, MESSAGE, MESSAGE],
        own[:1],
    )
    inputs = (cum, cum_t, q, k, v, grad, keep, got)

    def first(after):
        parts = (*near, from_left, from_right)
        return call(join_kernel, "join", scalars, parts, [WHOLE, WHOLE], after)

    def second(after, _):
        return call(inside_kernel, "inside", scalars, inputs, [narrow, wide, wide], after)

    keep_g, got_g, joined, (gq, gk, gv) = scan_blocks(scalars, mine_g, send_g, -1, (first, second))
    joined_r, joined_l = right(joined[0]), left(joined[1])
    gk, gv, order = call(
        finish_kernel,
        "finish",
        scalars,
        (cum, k, v, gk, gv, keep_g, got_g),
        [narrow, narrow, ((8, 128), F32)],
        far_outs=(0, 1),
        scratch=[pltpu.VMEM((512, 1024), BF16), pltpu.VMEM((512, 1024), BF16), pltpu.SemaphoreType.DMA((8,))],
    )
    (out,) = call(
        total_kernel,
        "total",
        scalars,
        (*own, joined_r, joined_l),
        [WHOLE],
        (order,),
        far_outs=(0,),
        scratch=[pltpu.VMEM((512, 1536), BF16), pltpu.SemaphoreType.DMA((4,))],
    )
    return out, gq, gk, gv


def solution(mesh):
    return jax.shard_map(
        body,
        mesh=mesh,
        in_specs=(
            P("seq", "head"),
            P("seq", "head"),
            P("seq", "head"),
            P("seq", "head"),
            P("head", None),
            P("seq", "head"),
        ),
        out_specs=(P("seq", "head"), P("seq", "head"), P("seq", "head"), P("seq", "head")),
        check_vma=False,
    )
```

```python
import functools

import jax
import jax.numpy as jnp
from jax import lax
from jax.experimental import pallas as pl
from jax.experimental.pallas import tpu as pltpu
from jax.sharding import PartitionSpec as P

EPS = 1e-05
F32 = jnp.float32
BF16 = jnp.bfloat16
MIB = 1024 * 1024
GIGA = 10**9

NN = (((1,), (0,)), ((), ()))
NT = (((1,), (1,)), ((), ()))
TN = (((0,), (0,)), ((), ()))


def dot(left, right, form=NN):
    return lax.dot_general(left, right, form, preferred_element_type=F32)


VMEM = pl.BlockSpec(memory_space=pltpu.VMEM)
SMEM = pl.BlockSpec(memory_space=pltpu.SMEM)
ANY = pl.BlockSpec(memory_space=pl.ANY)
HBM = pl.BlockSpec(memory_space=pltpu.HBM)


COST = dict(
    own_states=8 * GIGA,
    chip_total=0,
    local=0,
    meet=0,
    grad_own=0,
    arrive=0,
    split=0,
    halves=0,
    attend=0,
    grad_near=0,
    project_far=0,
    project_near=0,
    project_own=0,
    grad_far=0,
    join=0,
    inside=0,
    finish=0,
    total=0,
)


def call(kernel, name, scalars, args, outs, after=(), far=(), far_outs=(), scratch=(), room=12):
    count, waits = len(args), len(after)

    def run(*refs):
        kernel(*refs[: 1 + count], *refs[1 + count + waits :])

    return pl.pallas_call(
        run,
        out_shape=[jax.ShapeDtypeStruct(shape, dtype) for shape, dtype in outs],
        in_specs=[SMEM] + [HBM if i in far else VMEM for i in range(count)] + [ANY] * waits,
        out_specs=[HBM if i in far_outs else VMEM for i in range(len(outs))],
        scratch_shapes=list(scratch),
        compiler_params=pltpu.CompilerParams(vmem_limit_bytes=room * MIB),
        cost_estimate=pl.CostEstimate(flops=COST[name], bytes_accessed=0, transcendentals=0),
        name=name,
    )(scalars, *args, *after)


def three_terms(x):
    high = x.astype(BF16)
    rest = x - high.astype(F32)
    middle = rest.astype(BF16)
    low = (rest - middle.astype(F32)).astype(BF16)
    return high, middle, low


def head_columns(head):
    return slice(head * 128, head * 128 + 128)


def pack_decays(decays):
    high, middle, low = three_terms(decays)
    rows = [t.astype(F32) for t in (high, middle, low)]
    return jnp.concatenate(rows + [jnp.zeros_like(decays)], axis=0).astype(BF16)


def message_decays(ref):
    rows = ref[512:528, :].astype(F32)
    return rows[0:4] + rows[4:8] + rows[8:12]


MESSAGE = ((528, 128), BF16)
STATES = ((512, 128), BF16)
HALF = ((256, 1536), BF16)


def put_state(core, head, state, mine_ref, send_ref):
    rows = slice(head % 4 * 128, head % 4 * 128 + 128)
    here = core == head // 4

    @pl.when(here)
    def _():
        mine_ref[rows, :] = state

    @pl.when(jnp.logical_not(here))
    def _():
        send_ref[rows, :] = state


def put_decays(core, cum_t, mine_ref, send_ref):
    last = jnp.broadcast_to(cum_t[:, 511:512], (8, 128))
    swap = core == 1
    mine_ref[512:528, :] = pack_decays(jnp.where(swap, last[4:8], last[0:4]))
    send_ref[512:528, :] = pack_decays(jnp.where(swap, last[0:4], last[4:8]))


def state_kernel(
    s_ref,
    ld_ref,
    q_hbm,
    k_hbm,
    v_hbm,
    grad_hbm,
    cum_ref,
    cumt_ref,
    mine_ref,
    send_ref,
    q_ref,
    k_ref,
    v_ref,
    top_ref,
    bottom_ref,
    sems,
):
    core = s_ref[CORE]
    loads = []
    for part in range(4):
        cols = slice(part * 256, part * 256 + 256)
        pair = [
            pltpu.make_async_copy(far.at[:, cols], near.at[:, cols], sems.at[part * 2 + i])
            for i, (far, near) in enumerate(((k_hbm, k_ref), (v_hbm, v_ref)))
        ]
        for copy in pair:
            copy.start()
        loads.append(pair)
    late = [
        pltpu.make_async_copy(q_hbm, q_ref, sems.at[8]),
        pltpu.make_async_copy(grad_hbm.at[:256, :], top_ref, sems.at[9]),
        pltpu.make_async_copy(grad_hbm.at[256:, :], bottom_ref, sems.at[10]),
    ]
    for copy in late:
        copy.start()

    rows = lax.broadcasted_iota(jnp.int32, (512, 512), 0)
    cols = lax.broadcasted_iota(jnp.int32, (512, 512), 1)
    upper = jnp.where(rows <= cols, 1.0, 0.0).astype(BF16)
    lower = jnp.where(rows >= cols, 1.0, 0.0).astype(BF16)
    cum = jnp.zeros((512, 8), F32)
    cum_t = jnp.zeros((8, 512), F32)
    for term in three_terms(ld_ref[...])[::-1]:
        cum = cum + dot(lower, term, NT)
        cum_t = cum_t + dot(term, upper)
    cum_ref[...] = cum
    cumt_ref[...] = cum_t
    fall = jnp.exp(cum[511:512, :] - cum)
    for head in range(8):
        if head % 2 == 0:
            for copy in loads[head // 2]:
                copy.wait()
        at = head_columns(head)
        faded = (k_ref[:, at].astype(F32) * fall[:, head : head + 1]).astype(BF16)
        put_state(core, head, dot(faded, v_ref[:, at], TN).astype(BF16), mine_ref, send_ref)
    put_decays(core, cum_t, mine_ref, send_ref)
    for copy in late:
        copy.wait()


def own_states(scalars, logdecay_t, queries, keys, values, grad, after):
    held = ((512, 1024), BF16)
    return call(
        state_kernel,
        "own_states",
        scalars,
        (logdecay_t, queries, keys, values, grad),
        [((512, 8), F32), ((8, 512), F32), MESSAGE, MESSAGE, held, held, held, HALF, HALF],
        after,
        far=(1, 2, 3, 4),
        scratch=[pltpu.SemaphoreType.DMA((11,))],
        room=48,
    )


def chip_kernel(base, s_ref, mine_ref, got_ref, out_ref):
    first = s_ref[base] == 0
    d_mine, d_got = message_decays(mine_ref), message_decays(got_ref)
    w_mine = jnp.where(first, jnp.exp(d_got), 1.0)
    w_got = jnp.where(first, 1.0, jnp.exp(d_mine))
    for i in range(4):
        rows = slice(i * 128, i * 128 + 128)
        out_ref[rows, :] = (
            w_mine[i : i + 1] * mine_ref[rows, :].astype(F32) + w_got[i : i + 1] * got_ref[rows, :].astype(F32)
        ).astype(BF16)
    out_ref[512:528, :] = pack_decays(d_mine + d_got)


def meet_kernel(slot, s_ref, mine_ref, got_ref, *refs):
    prefix_in = refs[0] if len(refs) > 3 else None
    before_in = refs[1] if len(refs) > 3 else None
    total_ref, prefix_ref, before_ref = refs[-3:]
    later = s_ref[slot] == 1
    d_mine, d_got = message_decays(mine_ref), message_decays(got_ref)
    w_mine = jnp.where(later, 1.0, jnp.exp(d_got))
    w_got = jnp.where(later, jnp.exp(d_mine), 1.0)
    before = jnp.zeros((4, 128), F32) if before_in is None else before_in[0:4, :]
    reach = jnp.where(later, jnp.exp(before), 0.0)
    for i in range(4):
        rows = slice(i * 128, i * 128 + 128)
        mine, got = mine_ref[rows, :].astype(F32), got_ref[rows, :].astype(F32)
        total_ref[rows, :] = (w_mine[i : i + 1] * mine + w_got[i : i + 1] * got).astype(BF16)
        prefix = reach[i : i + 1] * got
        prefix_ref[rows, :] = prefix if prefix_in is None else prefix_in[rows, :] + prefix
    total_ref[512:528, :] = pack_decays(d_mine + d_got)
    before = before + jnp.where(later, d_got, 0.0)
    before_ref[...] = jnp.concatenate([before, before], axis=0)


def arrive_kernel(base, s_ref, last_ref, prefix_ref, before_ref, mine_ref, got_ref, keep_ref, send_ref):
    first = s_ref[base] == 0
    later = s_ref[base + 4] == 1
    reach = jnp.where(later, jnp.exp(before_ref[0:4, :]), 0.0)
    d_first = jnp.where(first, message_decays(mine_ref), message_decays(got_ref))
    w_first = jnp.exp(d_first)
    for i in range(4):
        rows = slice(i * 128, i * 128 + 128)
        at_first = prefix_ref[rows, :] + reach[i : i + 1] * last_ref[rows, :].astype(F32)
        state_first = jnp.where(first, mine_ref[rows, :].astype(F32), got_ref[rows, :].astype(F32))
        at_second = w_first[i : i + 1] * at_first + state_first
        keep_ref[rows, :] = jnp.where(first, at_first, at_second).astype(BF16)
        send_ref[rows, :] = jnp.where(first, at_second, at_first).astype(BF16)


SWAP = [(i, i ^ 1) for i in range(32)]
MEETINGS = [[(i, i ^ far) for i in range(32)] for far in (2, 4, 8, 16)]


def scan_blocks(scalars, mine, send, base, beside):
    got = lax.ppermute(send, "seq", SWAP)
    (total,) = call(functools.partial(chip_kernel, base), "chip_total", scalars, (mine, got), [MESSAGE])
    held = ()
    after = (total,)
    for turn in range(3):
        met = lax.ppermute(total, "seq", MEETINGS[turn])
        after = beside[turn](after)
        held = call(
            functools.partial(meet_kernel, base + 1 + turn),
            "meet",
            scalars,
            (total, met, *held),
            [MESSAGE, ((512, 128), F32), ((8, 128), F32)],
            after,
        )
        total, held = held[0], held[1:]
        after = (held[1],)
    met = lax.ppermute(total, "seq", MEETINGS[3])
    after = beside[3](after)
    keep, send_back = call(
        functools.partial(arrive_kernel, base),
        "arrive",
        scalars,
        (met, *held, mine, got),
        [STATES, STATES],
        after,
    )
    return keep, lax.ppermute(send_back, "seq", SWAP)


def decay_block(cum, cum_t, head, low, high):
    diff = cum[low:high, head : head + 1] - cum_t[head : head + 1, :high]
    rows = lax.broadcasted_iota(jnp.int32, diff.shape, 0) + low
    cols = lax.broadcasted_iota(jnp.int32, diff.shape, 1)
    return jnp.exp(jnp.where(rows >= cols, diff, -1e30))


def local_kernel(s_ref, cum_ref, cumt_ref, q_ref, k_ref, v_ref, w_hbm, out_ref, scaled_ref, turned_ref, w_ref, sems):
    loads = []
    for part in range(4):
        rows = slice(part * 256, part * 256 + 256)
        loads.append(pltpu.make_async_copy(w_hbm.at[rows, :], w_ref.at[rows, :], sems.at[part]))
        loads[-1].start()
    cum, cum_t = cum_ref[...], cumt_ref[...]
    rise = jnp.exp(cum)
    for head in range(8):
        at = head_columns(head)
        scaled = q_ref[:, at].astype(F32) * rise[:, head : head + 1]
        scaled_ref[:, at] = scaled.astype(BF16)
        turned_ref[at, :] = scaled.T.astype(BF16)
        for low in (0, 256):
            high = low + 256
            table = decay_block(cum, cum_t, head, low, high)
            probs = (dot(q_ref[low:high, at], k_ref[:high, at], NT) * table).astype(BF16)
            out_ref[low:high, at] = dot(probs, v_ref[:high, at])
    for copy in loads:
        copy.wait()


def local(scalars, cum, cum_t, q, k, v, weight, after):
    return call(
        local_kernel,
        "local",
        scalars,
        (cum, cum_t, q, k, v, weight),
        [((512, 1024), F32), ((512, 1024), BF16), ((1024, 512), BF16), ((1024, 6144), BF16)],
        after,
        far=(5,),
        room=34,
        scratch=[pltpu.SemaphoreType.DMA((4,))],
    )


def arrived(s_ref, head, keep_ref, got_ref):
    rows = slice(head % 4 * 128, head % 4 * 128 + 128)
    return jnp.where(s_ref[CORE] == head // 4, keep_ref[rows, :], got_ref[rows, :])


def attend_kernel(s_ref, local_ref, scaled_ref, keep_ref, got_ref, normed_ref, unit_ref, scale_ref):
    for head in range(8):
        at = head_columns(head)
        att = local_ref[:, at] + dot(scaled_ref[:, at], arrived(s_ref, head, keep_ref, got_ref))
        scale = lax.rsqrt(jnp.mean(att * att, axis=1, keepdims=True) + EPS)
        unit = att * scale
        unit_ref[:, at] = unit
        scale_ref[:, at] = jnp.broadcast_to(scale, unit.shape)
        normed_ref[:, at] = unit.astype(BF16)


WHOLE = ((512, 1536), BF16)
WIDE_HALF = ((256, 1536), F32)


OWN, NEAR_LEFT, NEAR_RIGHT, FAR, CORE = 10, 11, 12, 13, 14


def block_columns(s_ref, slot, offset=0, size=1536):
    return pl.ds(pl.multiple_of(s_ref[slot] * 1536 + offset, 128), size)


def products(s_ref, x_ref, w_ref, slot, top_ref, bottom_ref):
    for offset in (0, 512, 1024):
        out = dot(x_ref[...], w_ref[:, block_columns(s_ref, slot, offset, 512)])
        at = slice(offset, offset + 512)
        top_ref[:, at] = out[:256].astype(top_ref.dtype)
        bottom_ref[:, at] = out[256:].astype(bottom_ref.dtype)


def project_near_kernel(s_ref, x_ref, w_ref, right_top, right_bottom, left_top, left_bottom):
    products(s_ref, x_ref, w_ref, NEAR_RIGHT, right_top, right_bottom)
    products(s_ref, x_ref, w_ref, NEAR_LEFT, left_top, left_bottom)


def project_one_kernel(slot, s_ref, x_ref, w_ref, top_ref, bottom_ref):
    products(s_ref, x_ref, w_ref, slot, top_ref, bottom_ref)


def halves_kernel(s_ref, grad_hbm, top_ref, bottom_ref, order_ref, sems):
    order_ref[...] = jnp.zeros((8, 128), F32)
    copies = [
        pltpu.make_async_copy(grad_hbm.at[:256, :], top_ref, sems.at[0]),
        pltpu.make_async_copy(grad_hbm.at[256:, :], bottom_ref, sems.at[1]),
    ]
    for copy in copies:
        copy.start()
    for copy in copies:
        copy.wait()


def split_kernel(s_ref, a_ref, b_ref, top_ref, bottom_ref):
    top_ref[...] = a_ref[...]
    bottom_ref[...] = b_ref[...]


def join_kernel(s_ref, right_ref, from_left, left_ref, from_right, out_right, out_left):
    out_right[...] = (right_ref[...] + from_left[...].astype(F32)).astype(BF16)
    out_left[...] = (left_ref[...] + from_right[...].astype(F32)).astype(BF16)


def total_kernel(s_ref, top_ref, bottom_ref, top_a, top_b, bottom_a, bottom_b, out_ref, out_held, sems):
    copies = []
    for i, (own_ref, a_ref, b_ref) in enumerate(((top_ref, top_a, top_b), (bottom_ref, bottom_a, bottom_b))):
        for j in range(2):
            rows = slice(j * 128, j * 128 + 128)
            here = slice(i * 256 + j * 128, i * 256 + j * 128 + 128)
            total = own_ref[rows, :] + a_ref[rows, :].astype(F32) + b_ref[rows, :].astype(F32)
            out_held[here, :] = total.astype(BF16)
            copies.append(pltpu.make_async_copy(out_held.at[here, :], out_ref.at[here, :], sems.at[i * 2 + j]))
            copies[-1].start()
    for copy in copies:
        copy.wait()


def grad_own_kernel(s_ref, x_ref, w_ref, out_ref):
    for low in range(0, 1024, 256):
        rows = slice(low, low + 256)
        out_ref[:, rows] = dot(x_ref[...], w_ref[rows, block_columns(s_ref, OWN)], NT)


def grad_near_kernel(s_ref, a_top, a_bottom, b_top, b_bottom, w_ref, acc_ref, out_ref):
    a = jnp.concatenate([a_top[...], a_bottom[...]], axis=0)
    b = jnp.concatenate([b_top[...], b_bottom[...]], axis=0)
    for low in range(0, 1024, 256):
        rows = slice(low, low + 256)
        out_ref[:, rows] = (
            acc_ref[:, rows]
            + dot(a, w_ref[rows, block_columns(s_ref, NEAR_LEFT)], NT)
            + dot(b, w_ref[rows, block_columns(s_ref, NEAR_RIGHT)], NT)
        )


def grad_far_kernel(
    s_ref, c_ref, d_ref, w_ref, acc_ref, unit_ref, scale_ref, turned_ref, cumt_ref, grad_ref, mine_ref, send_ref
):
    core = s_ref[CORE]
    x = jnp.concatenate([c_ref[...], d_ref[...]], axis=0)
    for low in range(0, 1024, 256):
        rows = slice(low, low + 256)
        acc = acc_ref[:, rows] + dot(x, w_ref[rows, block_columns(s_ref, FAR)], NT)
        for i in range(2):
            head = low // 128 + i
            at = head_columns(head)
            unit, grad = unit_ref[:, at], acc[:, i * 128 : i * 128 + 128]
            along = jnp.mean(grad * unit, axis=1, keepdims=True)
            out = (scale_ref[:, at] * (grad - unit * along)).astype(BF16)
            grad_ref[:, at] = out
            put_state(core, head, dot(turned_ref[at, :], out).astype(BF16), mine_ref, send_ref)
    put_decays(core, cumt_ref[...], mine_ref, send_ref)


def inside_kernel(heads, s_ref, cum_ref, cumt_ref, q_ref, k_ref, v_ref, g_ref, keep_ref, got_ref, *refs):
    gq_ref, gk_ref, gv_ref = refs[-3:]
    cum, cum_t = cum_ref[...], cumt_ref[...]
    rise = jnp.exp(cum)
    if len(refs) > 3:
        gq_ref[:, :512] = refs[0][...]
    for head in heads:
        at = head_columns(head)
        to = head_columns(head - heads[0])
        to_q = at if len(refs) > 3 else to
        incoming = arrived(s_ref, head, keep_ref, got_ref)
        early_k = early_v = None
        for low in (0, 256):
            high = low + 256
            q, g = q_ref[low:high, at], g_ref[low:high, at]
            k, v = k_ref[:high, at], v_ref[:high, at]
            table = decay_block(cum, cum_t, head, low, high)
            probs = (dot(q, k, NT) * table).astype(BF16)
            scores = (dot(g, v, NT) * table).astype(BF16)
            gq = dot(scores, k) + rise[low:high, head : head + 1] * dot(g, incoming, NT)
            gq_ref[low:high, to_q] = gq.astype(BF16)
            part_k, part_v = dot(scores, q, TN), dot(probs, g, TN)
            if low == 0:
                early_k, early_v = part_k, part_v
            else:
                gk_ref[:256, to] = early_k + part_k[:256]
                gk_ref[256:, to] = part_k[256:]
                gv_ref[:256, to] = early_v + part_v[:256]
                gv_ref[256:, to] = part_v[256:]


def finish_kernel(
    s_ref, cum_ref, k_ref, v_ref, gk_a, gv_a, gk_b, gv_b, keep_ref, got_ref, gk_out, gv_out, order_ref, gk_held, gv_held, sems
):
    cum = cum_ref[...]
    fall = jnp.exp(cum[511:512, :] - cum)
    copies = []
    for head in range(8):
        at, part = head_columns(head), head_columns(head % 4)
        gk_ref, gv_ref = ((gk_a, gv_a), (gk_b, gv_b))[head // 4]
        outgoing = arrived(s_ref, head, keep_ref, got_ref)
        factor = fall[:, head : head + 1]
        gk_held[:, at] = (gk_ref[:, part] + factor * dot(v_ref[:, at], outgoing, NT)).astype(BF16)
        gv_held[:, at] = (gv_ref[:, part] + factor * dot(k_ref[:, at], outgoing)).astype(BF16)
        if head % 2 == 1:
            done = slice(head * 128 - 128, head * 128 + 128)
            for i, (held, out) in enumerate(((gk_held, gk_out), (gv_held, gv_out))):
                copies.append(pltpu.make_async_copy(held.at[:, done], out.at[:, done], sems.at[head - 1 + i]))
                copies[-1].start()
    order_ref[...] = jnp.zeros((8, 128), F32)
    for copy in copies:
        copy.wait()


RIGHT = [(i, (i + 1) % 4) for i in range(4)]
LEFT = [(i, (i + 3) % 4) for i in range(4)]


def body(queries, keys, values, logdecay, weight, output_gradient):
    at = lax.axis_index("seq").astype(jnp.int32)
    h = lax.axis_index("head").astype(jnp.int32)
    core, x, z = at % 2, at // 2 % 4, at // 8
    places = [core, x % 2, x // 2, z % 2, z // 2]
    blocks = [h, (h + 3) % 4, (h + 1) % 4, (h + 2) % 4, core]
    scalars = jnp.stack(places + [1 - place for place in places] + blocks).astype(jnp.int32)

    right = lambda a: lax.ppermute(a, "head", RIGHT)
    left = lambda a: lax.ppermute(a, "head", LEFT)
    wide, narrow = ((512, 1024), F32), ((512, 1024), BF16)

    top, bottom, order = call(
        halves_kernel,
        "halves",
        scalars,
        (output_gradient,),
        [HALF, HALF, ((8, 128), F32)],
        far=(0,),
        scratch=[pltpu.SemaphoreType.DMA((2,))],
        room=52,
    )
    a_top, b_bottom = right(top), left(bottom)
    cum, cum_t, mine, send, q, k, v, top, bottom = own_states(
        scalars, logdecay.T, queries, keys, values, output_gradient, (order,)
    )
    a_bottom, b_top = right(bottom), left(top)
    made = {}

    def make_local(after):
        made["local"] = local(scalars, cum, cum_t, q, k, v, weight, after)
        return made["local"][:1]

    def make_grad_own(after):
        w = made["local"][3]
        made["acc"] = call(grad_own_kernel, "grad_own", scalars, (output_gradient, w), [wide], after)[0]
        return (made["acc"],)

    def make_split(after):
        made["split"] = call(split_kernel, "split", scalars, (a_top, b_bottom), [HALF, HALF], after)
        return made["split"][:1]

    keep, got = scan_blocks(scalars, mine, send, 0, (make_local, make_grad_own, make_split, lambda after: after))
    local_part, scaled, turned, w = made["local"]
    acc = made["acc"]
    c, d = right(made["split"][0]), left(made["split"][1])
    normed, unit, scale = call(
        attend_kernel, "attend", scalars, (local_part, scaled, keep, got), [narrow, wide, wide]
    )

    (acc,) = call(grad_near_kernel, "grad_near", scalars, (a_top, a_bottom, b_top, b_bottom, w, acc), [wide], (unit,))
    far = call(functools.partial(project_one_kernel, FAR), "project_far", scalars, (normed, w), [HALF] * 2, (acc,))
    from_left, from_right = right(far[0]), left(far[1])
    near = call(
        project_near_kernel, "project_near", scalars, (normed, w), [WIDE_HALF, HALF, HALF, WIDE_HALF], far[:1]
    )
    grad, mine_g, send_g = call(
        grad_far_kernel,
        "grad_far",
        scalars,
        (c, d, w, acc, unit, scale, turned, cum_t),
        [narrow, MESSAGE, MESSAGE],
        near[:1],
    )
    inputs = (cum, cum_t, q, k, v, grad, keep, got)
    right_top, right_bottom, left_top, left_bottom = near
    direct_r, direct_l = right(right_bottom), left(left_top)

    def inside_first(after):
        made["a"] = call(
            functools.partial(inside_kernel, range(0, 4)),
            "inside",
            scalars,
            inputs,
            [((512, 512), BF16), ((512, 512), F32), ((512, 512), F32)],
            after,
        )
        return made["a"][:1]

    def inside_second(after):
        made["b"] = call(
            functools.partial(inside_kernel, range(4, 8)),
            "inside",
            scalars,
            inputs + (made["a"][0],),
            [narrow, ((512, 512), F32), ((512, 512), F32)],
            after,
        )
        return made["b"][1:2]

    def join(after):
        parts = (right_top, from_left, left_bottom, from_right)
        made["joined"] = call(join_kernel, "join", scalars, parts, [HALF, HALF], after)
        return made["joined"][:1]

    def project_own(after):
        one = functools.partial(project_one_kernel, OWN)
        made["own"] = call(one, "project_own", scalars, (normed, w), [WIDE_HALF] * 2, after)
        return made["own"][:1]

    keep_g, got_g = scan_blocks(scalars, mine_g, send_g, 5, (inside_first, join, inside_second, project_own))
    joined_r, joined_l = right(made["joined"][0]), left(made["joined"][1])
    gq = made["b"][0]
    gk, gv, order = call(
        finish_kernel,
        "finish",
        scalars,
        (cum, k, v, *made["a"][1:], *made["b"][1:], keep_g, got_g),
        [narrow, narrow, ((8, 128), F32)],
        far_outs=(0, 1),
        scratch=[pltpu.VMEM((512, 1024), BF16), pltpu.VMEM((512, 1024), BF16), pltpu.SemaphoreType.DMA((8,))],
    )
    (out,) = call(
        total_kernel,
        "total",
        scalars,
        (*made["own"], joined_r, direct_l, direct_r, joined_l),
        [WHOLE],
        (order,),
        far_outs=(0,),
        scratch=[pltpu.VMEM((512, 1536), BF16), pltpu.SemaphoreType.DMA((4,))],
    )
    return out, gq, gk, gv


def solution(mesh):
    return jax.shard_map(
        body,
        mesh=mesh,
        in_specs=(
            P("seq", "head"),
            P("seq", "head"),
            P("seq", "head"),
            P("seq", "head"),
            P("head", None),
            P("seq", "head"),
        ),
        out_specs=(P("seq", "head"), P("seq", "head"), P("seq", "head"), P("seq", "head")),
        check_vma=False,
    )
```

```python
import functools

import jax
import jax.numpy as jnp
from jax import lax
from jax.experimental import pallas as pl
from jax.experimental.pallas import tpu as pltpu
from jax.sharding import PartitionSpec as P

EPS = 1e-05
F32 = jnp.float32
BF16 = jnp.bfloat16
MIB = 1024 * 1024
GIGA = 10**9

NN = (((1,), (0,)), ((), ()))
NT = (((1,), (1,)), ((), ()))
TN = (((0,), (0,)), ((), ()))


def dot(left, right, form=NN):
    return lax.dot_general(left, right, form, preferred_element_type=F32)


VMEM = pl.BlockSpec(memory_space=pltpu.VMEM)
SMEM = pl.BlockSpec(memory_space=pltpu.SMEM)
ANY = pl.BlockSpec(memory_space=pl.ANY)
HBM = pl.BlockSpec(memory_space=pltpu.HBM)


COST = dict(
    own_states=8 * GIGA,
    chip_total=0,
    local=0,
    meet=0,
    grad_own=0,
    arrive=0,
    split=0,
    halves=0,
    attend=0,
    grad_near=0,
    project_far=0,
    project_near=0,
    project_own=0,
    grad_far=0,
    join=0,
    add_direct=0,
    inside=0,
    finish=0,
    total=0,
)


def call(kernel, name, scalars, args, outs, after=(), far=(), far_outs=(), scratch=(), room=12):
    count, waits = len(args), len(after)

    def run(*refs):
        kernel(*refs[: 1 + count], *refs[1 + count + waits :])

    return pl.pallas_call(
        run,
        out_shape=[jax.ShapeDtypeStruct(shape, dtype) for shape, dtype in outs],
        in_specs=[SMEM] + [HBM if i in far else VMEM for i in range(count)] + [ANY] * waits,
        out_specs=[HBM if i in far_outs else VMEM for i in range(len(outs))],
        scratch_shapes=list(scratch),
        compiler_params=pltpu.CompilerParams(vmem_limit_bytes=room * MIB),
        cost_estimate=pl.CostEstimate(flops=COST[name], bytes_accessed=0, transcendentals=0),
        name=name,
    )(scalars, *args, *after)


def three_terms(x):
    high = x.astype(BF16)
    rest = x - high.astype(F32)
    middle = rest.astype(BF16)
    low = (rest - middle.astype(F32)).astype(BF16)
    return high, middle, low


def head_columns(head):
    return slice(head * 128, head * 128 + 128)


def pack_decays(decays):
    high, middle, low = three_terms(decays)
    rows = [t.astype(F32) for t in (high, middle, low)]
    return jnp.concatenate(rows + [jnp.zeros_like(decays)], axis=0).astype(BF16)


def message_decays(ref):
    rows = ref[512:528, :].astype(F32)
    return rows[0:4] + rows[4:8] + rows[8:12]


MESSAGE = ((528, 128), BF16)
STATES = ((512, 128), BF16)
HALF = ((256, 1536), BF16)


def put_state(core, head, state, mine_ref, send_ref):
    rows = slice(head % 4 * 128, head % 4 * 128 + 128)
    here = core == head // 4

    @pl.when(here)
    def _():
        mine_ref[rows, :] = state

    @pl.when(jnp.logical_not(here))
    def _():
        send_ref[rows, :] = state


def put_decays(core, cum_t, mine_ref, send_ref):
    last = jnp.broadcast_to(cum_t[:, 511:512], (8, 128))
    swap = core == 1
    mine_ref[512:528, :] = pack_decays(jnp.where(swap, last[4:8], last[0:4]))
    send_ref[512:528, :] = pack_decays(jnp.where(swap, last[0:4], last[4:8]))


def state_kernel(
    s_ref,
    ld_ref,
    q_hbm,
    k_hbm,
    v_hbm,
    grad_hbm,
    cum_ref,
    cumt_ref,
    mine_ref,
    send_ref,
    q_ref,
    k_ref,
    v_ref,
    top_ref,
    bottom_ref,
    sems,
):
    core = s_ref[CORE]
    loads = []
    for part in range(4):
        cols = slice(part * 256, part * 256 + 256)
        pair = [
            pltpu.make_async_copy(far.at[:, cols], near.at[:, cols], sems.at[part * 2 + i])
            for i, (far, near) in enumerate(((k_hbm, k_ref), (v_hbm, v_ref)))
        ]
        for copy in pair:
            copy.start()
        loads.append(pair)
    late = [
        pltpu.make_async_copy(q_hbm, q_ref, sems.at[8]),
        pltpu.make_async_copy(grad_hbm.at[:256, :], top_ref, sems.at[9]),
        pltpu.make_async_copy(grad_hbm.at[256:, :], bottom_ref, sems.at[10]),
    ]
    for copy in late:
        copy.start()

    rows = lax.broadcasted_iota(jnp.int32, (512, 512), 0)
    cols = lax.broadcasted_iota(jnp.int32, (512, 512), 1)
    upper = jnp.where(rows <= cols, 1.0, 0.0).astype(BF16)
    lower = jnp.where(rows >= cols, 1.0, 0.0).astype(BF16)
    cum = jnp.zeros((512, 8), F32)
    cum_t = jnp.zeros((8, 512), F32)
    for term in three_terms(ld_ref[...])[::-1]:
        cum = cum + dot(lower, term, NT)
        cum_t = cum_t + dot(term, upper)
    cum_ref[...] = cum
    cumt_ref[...] = cum_t
    fall = jnp.exp(cum[511:512, :] - cum)
    for head in range(8):
        if head % 2 == 0:
            for copy in loads[head // 2]:
                copy.wait()
        at = head_columns(head)
        faded = (k_ref[:, at].astype(F32) * fall[:, head : head + 1]).astype(BF16)
        put_state(core, head, dot(faded, v_ref[:, at], TN).astype(BF16), mine_ref, send_ref)
    put_decays(core, cum_t, mine_ref, send_ref)
    for copy in late:
        copy.wait()


def own_states(scalars, logdecay_t, queries, keys, values, grad, after):
    held = ((512, 1024), BF16)
    return call(
        state_kernel,
        "own_states",
        scalars,
        (logdecay_t, queries, keys, values, grad),
        [((512, 8), F32), ((8, 512), F32), MESSAGE, MESSAGE, held, held, held, HALF, HALF],
        after,
        far=(1, 2, 3, 4),
        scratch=[pltpu.SemaphoreType.DMA((11,))],
        room=48,
    )


def chip_kernel(base, s_ref, mine_ref, got_ref, out_ref):
    first = s_ref[base] == 0
    d_mine, d_got = message_decays(mine_ref), message_decays(got_ref)
    w_mine = jnp.where(first, jnp.exp(d_got), 1.0)
    w_got = jnp.where(first, 1.0, jnp.exp(d_mine))
    for i in range(4):
        rows = slice(i * 128, i * 128 + 128)
        out_ref[rows, :] = (
            w_mine[i : i + 1] * mine_ref[rows, :].astype(F32) + w_got[i : i + 1] * got_ref[rows, :].astype(F32)
        ).astype(BF16)
    out_ref[512:528, :] = pack_decays(d_mine + d_got)


def meet_kernel(slot, s_ref, mine_ref, got_ref, *refs):
    prefix_in = refs[0] if len(refs) > 3 else None
    before_in = refs[1] if len(refs) > 3 else None
    total_ref, prefix_ref, before_ref = refs[-3:]
    later = s_ref[slot] == 1
    d_mine, d_got = message_decays(mine_ref), message_decays(got_ref)
    w_mine = jnp.where(later, 1.0, jnp.exp(d_got))
    w_got = jnp.where(later, jnp.exp(d_mine), 1.0)
    before = jnp.zeros((4, 128), F32) if before_in is None else before_in[0:4, :]
    reach = jnp.where(later, jnp.exp(before), 0.0)
    for i in range(4):
        rows = slice(i * 128, i * 128 + 128)
        mine, got = mine_ref[rows, :].astype(F32), got_ref[rows, :].astype(F32)
        total_ref[rows, :] = (w_mine[i : i + 1] * mine + w_got[i : i + 1] * got).astype(BF16)
        prefix = reach[i : i + 1] * got
        prefix_ref[rows, :] = prefix if prefix_in is None else prefix_in[rows, :] + prefix
    total_ref[512:528, :] = pack_decays(d_mine + d_got)
    before = before + jnp.where(later, d_got, 0.0)
    before_ref[...] = jnp.concatenate([before, before], axis=0)


def arrive_kernel(base, s_ref, last_ref, prefix_ref, before_ref, mine_ref, got_ref, keep_ref, send_ref):
    first = s_ref[base] == 0
    later = s_ref[base + 4] == 1
    reach = jnp.where(later, jnp.exp(before_ref[0:4, :]), 0.0)
    d_first = jnp.where(first, message_decays(mine_ref), message_decays(got_ref))
    w_first = jnp.exp(d_first)
    for i in range(4):
        rows = slice(i * 128, i * 128 + 128)
        at_first = prefix_ref[rows, :] + reach[i : i + 1] * last_ref[rows, :].astype(F32)
        state_first = jnp.where(first, mine_ref[rows, :].astype(F32), got_ref[rows, :].astype(F32))
        at_second = w_first[i : i + 1] * at_first + state_first
        keep_ref[rows, :] = jnp.where(first, at_first, at_second).astype(BF16)
        send_ref[rows, :] = jnp.where(first, at_second, at_first).astype(BF16)


SWAP = [(i, i ^ 1) for i in range(32)]
MEETINGS = [[(i, i ^ far) for i in range(32)] for far in (2, 4, 8, 16)]


def scan_blocks(scalars, mine, send, base, beside):
    got = lax.ppermute(send, "seq", SWAP)
    (total,) = call(functools.partial(chip_kernel, base), "chip_total", scalars, (mine, got), [MESSAGE])
    held = ()
    after = (total,)
    for turn in range(3):
        met = lax.ppermute(total, "seq", MEETINGS[turn])
        after = beside[turn](after)
        held = call(
            functools.partial(meet_kernel, base + 1 + turn),
            "meet",
            scalars,
            (total, met, *held),
            [MESSAGE, ((512, 128), F32), ((8, 128), F32)],
            after,
        )
        total, held = held[0], held[1:]
        after = (held[1],)
    met = lax.ppermute(total, "seq", MEETINGS[3])
    after = beside[3](after)
    keep, send_back = call(
        functools.partial(arrive_kernel, base),
        "arrive",
        scalars,
        (met, *held, mine, got),
        [STATES, STATES],
        after,
    )
    return keep, lax.ppermute(send_back, "seq", SWAP)


def decay_block(cum, cum_t, head, low, high):
    diff = cum[low:high, head : head + 1] - cum_t[head : head + 1, :high]
    rows = lax.broadcasted_iota(jnp.int32, diff.shape, 0) + low
    cols = lax.broadcasted_iota(jnp.int32, diff.shape, 1)
    return jnp.exp(jnp.where(rows >= cols, diff, -1e30))


def local_kernel(s_ref, cum_ref, cumt_ref, q_ref, k_ref, v_ref, w_hbm, out_ref, scaled_ref, turned_ref, w_ref, sems):
    loads = []
    for part in range(4):
        rows = slice(part * 256, part * 256 + 256)
        loads.append(pltpu.make_async_copy(w_hbm.at[rows, :], w_ref.at[rows, :], sems.at[part]))
        loads[-1].start()
    cum, cum_t = cum_ref[...], cumt_ref[...]
    rise = jnp.exp(cum)
    for head in range(8):
        at = head_columns(head)
        scaled = q_ref[:, at].astype(F32) * rise[:, head : head + 1]
        scaled_ref[:, at] = scaled.astype(BF16)
        turned_ref[at, :] = scaled.T.astype(BF16)
        for low in (0, 256):
            high = low + 256
            table = decay_block(cum, cum_t, head, low, high)
            probs = (dot(q_ref[low:high, at], k_ref[:high, at], NT) * table).astype(BF16)
            out_ref[low:high, at] = dot(probs, v_ref[:high, at])
    for copy in loads:
        copy.wait()


def local(scalars, cum, cum_t, q, k, v, weight, after):
    return call(
        local_kernel,
        "local",
        scalars,
        (cum, cum_t, q, k, v, weight),
        [((512, 1024), F32), ((512, 1024), BF16), ((1024, 512), BF16), ((1024, 6144), BF16)],
        after,
        far=(5,),
        room=34,
        scratch=[pltpu.SemaphoreType.DMA((4,))],
    )


def arrived(s_ref, head, keep_ref, got_ref):
    rows = slice(head % 4 * 128, head % 4 * 128 + 128)
    return jnp.where(s_ref[CORE] == head // 4, keep_ref[rows, :], got_ref[rows, :])


def attend_kernel(s_ref, local_ref, scaled_ref, keep_ref, got_ref, normed_ref, unit_ref, scale_ref):
    for head in range(8):
        at = head_columns(head)
        att = local_ref[:, at] + dot(scaled_ref[:, at], arrived(s_ref, head, keep_ref, got_ref))
        scale = lax.rsqrt(jnp.mean(att * att, axis=1, keepdims=True) + EPS)
        unit = att * scale
        unit_ref[:, at] = unit
        scale_ref[:, at] = jnp.broadcast_to(scale, unit.shape)
        normed_ref[:, at] = unit.astype(BF16)


WHOLE = ((512, 1536), BF16)
WIDE_HALF = ((256, 1536), F32)


OWN, NEAR_LEFT, NEAR_RIGHT, FAR, CORE = 10, 11, 12, 13, 14


def block_columns(s_ref, slot, offset=0, size=1536):
    return pl.ds(pl.multiple_of(s_ref[slot] * 1536 + offset, 128), size)


def products(s_ref, x_ref, w_ref, slot, top_ref, bottom_ref):
    for offset in (0, 512, 1024):
        out = dot(x_ref[...], w_ref[:, block_columns(s_ref, slot, offset, 512)])
        at = slice(offset, offset + 512)
        top_ref[:, at] = out[:256].astype(top_ref.dtype)
        bottom_ref[:, at] = out[256:].astype(bottom_ref.dtype)


def project_near_kernel(s_ref, x_ref, w_ref, right_top, right_bottom, left_top, left_bottom):
    products(s_ref, x_ref, w_ref, NEAR_RIGHT, right_top, right_bottom)
    products(s_ref, x_ref, w_ref, NEAR_LEFT, left_top, left_bottom)


def project_one_kernel(slot, s_ref, x_ref, w_ref, top_ref, bottom_ref):
    products(s_ref, x_ref, w_ref, slot, top_ref, bottom_ref)


def halves_kernel(s_ref, grad_hbm, top_ref, bottom_ref, order_ref, sems):
    order_ref[...] = jnp.zeros((8, 128), F32)
    copies = [
        pltpu.make_async_copy(grad_hbm.at[:256, :], top_ref, sems.at[0]),
        pltpu.make_async_copy(grad_hbm.at[256:, :], bottom_ref, sems.at[1]),
    ]
    for copy in copies:
        copy.start()
    for copy in copies:
        copy.wait()


def split_kernel(s_ref, a_ref, b_ref, top_ref, bottom_ref):
    top_ref[...] = a_ref[...]
    bottom_ref[...] = b_ref[...]


def join_kernel(s_ref, right_ref, from_left, left_ref, from_right, out_right, out_left):
    out_right[...] = (right_ref[...] + from_left[...].astype(F32)).astype(BF16)
    out_left[...] = (left_ref[...] + from_right[...].astype(F32)).astype(BF16)


def add_direct_kernel(s_ref, top_ref, bottom_ref, from_right, from_left, top_out, bottom_out):
    top_out[...] = top_ref[...] + from_right[...].astype(F32)
    bottom_out[...] = bottom_ref[...] + from_left[...].astype(F32)


def total_kernel(s_ref, top_ref, bottom_ref, from_left, from_right, out_ref, out_held, sems):
    copies = []
    for i, (own_ref, a_ref) in enumerate(((top_ref, from_left), (bottom_ref, from_right))):
        for j in range(2):
            rows = slice(j * 128, j * 128 + 128)
            here = slice(i * 256 + j * 128, i * 256 + j * 128 + 128)
            total = own_ref[rows, :] + a_ref[rows, :].astype(F32)
            out_held[here, :] = total.astype(BF16)
            copies.append(pltpu.make_async_copy(out_held.at[here, :], out_ref.at[here, :], sems.at[i * 2 + j]))
            copies[-1].start()
    for copy in copies:
        copy.wait()


def grad_own_kernel(s_ref, x_ref, w_ref, out_ref):
    for low in range(0, 1024, 256):
        rows = slice(low, low + 256)
        out_ref[:, rows] = dot(x_ref[...], w_ref[rows, block_columns(s_ref, OWN)], NT)


def grad_near_kernel(s_ref, a_top, a_bottom, b_top, b_bottom, w_ref, acc_ref, out_ref):
    a = jnp.concatenate([a_top[...], a_bottom[...]], axis=0)
    b = jnp.concatenate([b_top[...], b_bottom[...]], axis=0)
    for low in range(0, 1024, 256):
        rows = slice(low, low + 256)
        out_ref[:, rows] = (
            acc_ref[:, rows]
            + dot(a, w_ref[rows, block_columns(s_ref, NEAR_LEFT)], NT)
            + dot(b, w_ref[rows, block_columns(s_ref, NEAR_RIGHT)], NT)
        )


def grad_far_kernel(
    s_ref, c_ref, d_ref, w_ref, acc_ref, unit_ref, scale_ref, turned_ref, cumt_ref, grad_ref, mine_ref, send_ref
):
    core = s_ref[CORE]
    x = jnp.concatenate([c_ref[...], d_ref[...]], axis=0)
    for low in range(0, 1024, 256):
        rows = slice(low, low + 256)
        acc = acc_ref[:, rows] + dot(x, w_ref[rows, block_columns(s_ref, FAR)], NT)
        for i in range(2):
            head = low // 128 + i
            at = head_columns(head)
            unit, grad = unit_ref[:, at], acc[:, i * 128 : i * 128 + 128]
            along = jnp.mean(grad * unit, axis=1, keepdims=True)
            out = (scale_ref[:, at] * (grad - unit * along)).astype(BF16)
            grad_ref[:, at] = out
            put_state(core, head, dot(turned_ref[at, :], out).astype(BF16), mine_ref, send_ref)
    put_decays(core, cumt_ref[...], mine_ref, send_ref)


def inside_kernel(heads, s_ref, cum_ref, cumt_ref, q_ref, k_ref, v_ref, g_ref, keep_ref, got_ref, *refs):
    gq_ref, gk_ref, gv_ref = refs[-3:]
    cum, cum_t = cum_ref[...], cumt_ref[...]
    rise = jnp.exp(cum)
    if len(refs) > 3:
        gq_ref[:, :512] = refs[0][...]
    for head in heads:
        at = head_columns(head)
        to = head_columns(head - heads[0])
        to_q = at if len(refs) > 3 else to
        incoming = arrived(s_ref, head, keep_ref, got_ref)
        early_k = early_v = None
        for low in (0, 256):
            high = low + 256
            q, g = q_ref[low:high, at], g_ref[low:high, at]
            k, v = k_ref[:high, at], v_ref[:high, at]
            table = decay_block(cum, cum_t, head, low, high)
            probs = (dot(q, k, NT) * table).astype(BF16)
            scores = (dot(g, v, NT) * table).astype(BF16)
            gq = dot(scores, k) + rise[low:high, head : head + 1] * dot(g, incoming, NT)
            gq_ref[low:high, to_q] = gq.astype(BF16)
            part_k, part_v = dot(scores, q, TN), dot(probs, g, TN)
            if low == 0:
                early_k, early_v = part_k, part_v
            else:
                gk_ref[:256, to] = early_k + part_k[:256]
                gk_ref[256:, to] = part_k[256:]
                gv_ref[:256, to] = early_v + part_v[:256]
                gv_ref[256:, to] = part_v[256:]


def finish_kernel(
    s_ref, cum_ref, k_ref, v_ref, gk_a, gv_a, gk_b, gv_b, keep_ref, got_ref, gk_out, gv_out, order_ref, gk_held, gv_held, sems
):
    cum = cum_ref[...]
    fall = jnp.exp(cum[511:512, :] - cum)
    copies = []
    for head in range(8):
        at, part = head_columns(head), head_columns(head % 4)
        gk_ref, gv_ref = ((gk_a, gv_a), (gk_b, gv_b))[head // 4]
        outgoing = arrived(s_ref, head, keep_ref, got_ref)
        factor = fall[:, head : head + 1]
        gk_held[:, at] = (gk_ref[:, part] + factor * dot(v_ref[:, at], outgoing, NT)).astype(BF16)
        gv_held[:, at] = (gv_ref[:, part] + factor * dot(k_ref[:, at], outgoing)).astype(BF16)
        if head % 2 == 1:
            done = slice(head * 128 - 128, head * 128 + 128)
            for i, (held, out) in enumerate(((gk_held, gk_out), (gv_held, gv_out))):
                copies.append(pltpu.make_async_copy(held.at[:, done], out.at[:, done], sems.at[head - 1 + i]))
                copies[-1].start()
    order_ref[...] = jnp.zeros((8, 128), F32)
    for copy in copies:
        copy.wait()


RIGHT = [(i, (i + 1) % 4) for i in range(4)]
LEFT = [(i, (i + 3) % 4) for i in range(4)]


def body(queries, keys, values, logdecay, weight, output_gradient):
    at = lax.axis_index("seq").astype(jnp.int32)
    h = lax.axis_index("head").astype(jnp.int32)
    core, x, z = at % 2, at // 2 % 4, at // 8
    places = [core, x % 2, x // 2, z % 2, z // 2]
    blocks = [h, (h + 3) % 4, (h + 1) % 4, (h + 2) % 4, core]
    scalars = jnp.stack(places + [1 - place for place in places] + blocks).astype(jnp.int32)

    right = lambda a: lax.ppermute(a, "head", RIGHT)
    left = lambda a: lax.ppermute(a, "head", LEFT)
    wide, narrow = ((512, 1024), F32), ((512, 1024), BF16)

    top, bottom, order = call(
        halves_kernel,
        "halves",
        scalars,
        (output_gradient,),
        [HALF, HALF, ((8, 128), F32)],
        far=(0,),
        scratch=[pltpu.SemaphoreType.DMA((2,))],
        room=52,
    )
    a_top, b_bottom = right(top), left(bottom)
    cum, cum_t, mine, send, q, k, v, top, bottom = own_states(
        scalars, logdecay.T, queries, keys, values, output_gradient, (order,)
    )
    a_bottom, b_top = right(bottom), left(top)
    made = {}

    def make_local(after):
        made["local"] = local(scalars, cum, cum_t, q, k, v, weight, after)
        return made["local"][:1]

    def make_grad_own(after):
        w = made["local"][3]
        made["acc"] = call(grad_own_kernel, "grad_own", scalars, (output_gradient, w), [wide], after)[0]
        return (made["acc"],)

    def make_split(after):
        made["split"] = call(split_kernel, "split", scalars, (a_top, b_bottom), [HALF, HALF], after)
        return made["split"][:1]

    keep, got = scan_blocks(scalars, mine, send, 0, (make_local, make_grad_own, make_split, lambda after: after))
    local_part, scaled, turned, w = made["local"]
    acc = made["acc"]
    c, d = right(made["split"][0]), left(made["split"][1])
    normed, unit, scale = call(
        attend_kernel, "attend", scalars, (local_part, scaled, keep, got), [narrow, wide, wide]
    )

    (acc,) = call(grad_near_kernel, "grad_near", scalars, (a_top, a_bottom, b_top, b_bottom, w, acc), [wide], (unit,))
    far = call(functools.partial(project_one_kernel, FAR), "project_far", scalars, (normed, w), [HALF] * 2, (acc,))
    from_left, from_right = right(far[0]), left(far[1])
    near = call(
        project_near_kernel, "project_near", scalars, (normed, w), [WIDE_HALF, HALF, HALF, WIDE_HALF], far[:1]
    )
    grad, mine_g, send_g = call(
        grad_far_kernel,
        "grad_far",
        scalars,
        (c, d, w, acc, unit, scale, turned, cum_t),
        [narrow, MESSAGE, MESSAGE],
        near[:1],
    )
    inputs = (cum, cum_t, q, k, v, grad, keep, got)
    right_top, right_bottom, left_top, left_bottom = near
    direct_r, direct_l = right(right_bottom), left(left_top)

    def inside_first(after):
        made["a"] = call(
            functools.partial(inside_kernel, range(0, 4)),
            "inside",
            scalars,
            inputs,
            [((512, 512), BF16), ((512, 512), F32), ((512, 512), F32)],
            after,
        )
        return made["a"][:1]

    def inside_second(after):
        made["b"] = call(
            functools.partial(inside_kernel, range(4, 8)),
            "inside",
            scalars,
            inputs + (made["a"][0],),
            [narrow, ((512, 512), F32), ((512, 512), F32)],
            after,
        )
        return made["b"][1:2]

    def join(after):
        parts = (right_top, from_left, left_bottom, from_right)
        made["joined"] = call(join_kernel, "join", scalars, parts, [HALF, HALF], after)
        return made["joined"][:1]

    def project_own(after):
        one = functools.partial(project_one_kernel, OWN)
        made["own"] = call(one, "project_own", scalars, (normed, w), [WIDE_HALF] * 2, after)
        return made["own"][:1]

    def add_direct(after):
        parts = (*made["own"], direct_l, direct_r)
        made["own"] = call(add_direct_kernel, "add_direct", scalars, parts, [WIDE_HALF] * 2, after)
        return made["own"][:1]

    turns = (
        inside_first,
        lambda after: project_own(join(after)),
        lambda after: add_direct(inside_second(after)),
        lambda after: after,
    )
    keep_g, got_g = scan_blocks(scalars, mine_g, send_g, 5, turns)
    joined_r, joined_l = right(made["joined"][0]), left(made["joined"][1])
    gq = made["b"][0]
    gk, gv, order = call(
        finish_kernel,
        "finish",
        scalars,
        (cum, k, v, *made["a"][1:], *made["b"][1:], keep_g, got_g),
        [narrow, narrow, ((8, 128), F32)],
        far_outs=(0, 1),
        scratch=[pltpu.VMEM((512, 1024), BF16), pltpu.VMEM((512, 1024), BF16), pltpu.SemaphoreType.DMA((8,))],
    )
    (out,) = call(
        total_kernel,
        "total",
        scalars,
        (*made["own"], joined_r, joined_l),
        [WHOLE],
        (order,),
        far_outs=(0,),
        scratch=[pltpu.VMEM((512, 1536), BF16), pltpu.SemaphoreType.DMA((4,))],
    )
    return out, gq, gk, gv


def solution(mesh):
    return jax.shard_map(
        body,
        mesh=mesh,
        in_specs=(
            P("seq", "head"),
            P("seq", "head"),
            P("seq", "head"),
            P("seq", "head"),
            P("head", None),
            P("seq", "head"),
        ),
        out_specs=(P("seq", "head"), P("seq", "head"), P("seq", "head"), P("seq", "head")),
        check_vma=False,
    )
```

```python
import functools

import jax
import jax.numpy as jnp
from jax import lax
from jax.experimental import pallas as pl
from jax.experimental.pallas import tpu as pltpu
from jax.sharding import PartitionSpec as P

EPS = 1e-05
F32 = jnp.float32
BF16 = jnp.bfloat16
MIB = 1024 * 1024
GIGA = 10**9

NN = (((1,), (0,)), ((), ()))
NT = (((1,), (1,)), ((), ()))
TN = (((0,), (0,)), ((), ()))


def dot(left, right, form=NN):
    return lax.dot_general(left, right, form, preferred_element_type=F32)


VMEM = pl.BlockSpec(memory_space=pltpu.VMEM)
SMEM = pl.BlockSpec(memory_space=pltpu.SMEM)
ANY = pl.BlockSpec(memory_space=pl.ANY)
HBM = pl.BlockSpec(memory_space=pltpu.HBM)


COST = dict(
    own_states=8 * GIGA,
    chip_total=0,
    local=0,
    meet=0,
    grad_own=0,
    arrive=0,
    split=0,
    halves=0,
    attend=0,
    grad_near=0,
    project_far=0,
    project_near=0,
    project_own=0,
    grad_far=0,
    join=0,
    add_direct=0,
    inside=0,
    finish=0,
    total=0,
)


def call(kernel, name, scalars, args, outs, after=(), far=(), far_outs=(), scratch=(), room=12):
    count, waits = len(args), len(after)
    lead = () if scalars is None else (scalars,)

    def run(*refs):
        refs = refs if lead else (None, *refs)
        kernel(*refs[: 1 + count], *refs[1 + count + waits :])

    return pl.pallas_call(
        run,
        out_shape=[jax.ShapeDtypeStruct(shape, dtype) for shape, dtype in outs],
        in_specs=[SMEM] * len(lead) + [HBM if i in far else VMEM for i in range(count)] + [ANY] * waits,
        out_specs=[HBM if i in far_outs else VMEM for i in range(len(outs))],
        scratch_shapes=list(scratch),
        compiler_params=pltpu.CompilerParams(vmem_limit_bytes=room * MIB),
        cost_estimate=pl.CostEstimate(flops=COST[name], bytes_accessed=0, transcendentals=0),
        name=name,
    )(*lead, *args, *after)


def three_terms(x):
    high = x.astype(BF16)
    rest = x - high.astype(F32)
    middle = rest.astype(BF16)
    low = (rest - middle.astype(F32)).astype(BF16)
    return high, middle, low


def head_columns(head):
    return slice(head * 128, head * 128 + 128)


def pack_decays(decays):
    high, middle, low = three_terms(decays)
    rows = [t.astype(F32) for t in (high, middle, low)]
    return jnp.concatenate(rows + [jnp.zeros_like(decays)], axis=0).astype(BF16)


def message_decays(ref):
    rows = ref[512:528, :].astype(F32)
    return rows[0:4] + rows[4:8] + rows[8:12]


MESSAGE = ((528, 128), BF16)
STATES = ((512, 128), BF16)
HALF = ((256, 1536), BF16)


def put_state(core, head, state, mine_ref, send_ref):
    rows = slice(head % 4 * 128, head % 4 * 128 + 128)
    here = core == head // 4

    @pl.when(here)
    def _():
        mine_ref[rows, :] = state

    @pl.when(jnp.logical_not(here))
    def _():
        send_ref[rows, :] = state


def put_decays(core, cum_t, mine_ref, send_ref):
    last = jnp.broadcast_to(cum_t[:, 511:512], (8, 128))
    swap = core == 1
    mine_ref[512:528, :] = pack_decays(jnp.where(swap, last[4:8], last[0:4]))
    send_ref[512:528, :] = pack_decays(jnp.where(swap, last[0:4], last[4:8]))


def state_kernel(
    s_ref,
    ld_ref,
    q_hbm,
    k_hbm,
    v_hbm,
    grad_hbm,
    cum_ref,
    cumt_ref,
    mine_ref,
    send_ref,
    q_ref,
    k_ref,
    v_ref,
    top_ref,
    bottom_ref,
    sems,
):
    core = s_ref[CORE]
    loads = []
    for part in range(4):
        cols = slice(part * 256, part * 256 + 256)
        pair = [
            pltpu.make_async_copy(far.at[:, cols], near.at[:, cols], sems.at[part * 2 + i])
            for i, (far, near) in enumerate(((k_hbm, k_ref), (v_hbm, v_ref)))
        ]
        for copy in pair:
            copy.start()
        loads.append(pair)
    late = [
        pltpu.make_async_copy(q_hbm, q_ref, sems.at[8]),
        pltpu.make_async_copy(grad_hbm.at[:256, :], top_ref, sems.at[9]),
        pltpu.make_async_copy(grad_hbm.at[256:, :], bottom_ref, sems.at[10]),
    ]
    for copy in late:
        copy.start()

    rows = lax.broadcasted_iota(jnp.int32, (512, 512), 0)
    cols = lax.broadcasted_iota(jnp.int32, (512, 512), 1)
    upper = jnp.where(rows <= cols, 1.0, 0.0).astype(BF16)
    lower = jnp.where(rows >= cols, 1.0, 0.0).astype(BF16)
    cum = jnp.zeros((512, 8), F32)
    cum_t = jnp.zeros((8, 512), F32)
    for term in three_terms(ld_ref[...])[::-1]:
        cum = cum + dot(lower, term, NT)
        cum_t = cum_t + dot(term, upper)
    cum_ref[...] = cum
    cumt_ref[...] = cum_t
    fall = jnp.exp(cum[511:512, :] - cum)
    for head in range(8):
        if head % 2 == 0:
            for copy in loads[head // 2]:
                copy.wait()
        at = head_columns(head)
        faded = (k_ref[:, at].astype(F32) * fall[:, head : head + 1]).astype(BF16)
        put_state(core, head, dot(faded, v_ref[:, at], TN).astype(BF16), mine_ref, send_ref)
    put_decays(core, cum_t, mine_ref, send_ref)
    for copy in late:
        copy.wait()


def own_states(scalars, logdecay_t, queries, keys, values, grad, after):
    held = ((512, 1024), BF16)
    return call(
        state_kernel,
        "own_states",
        scalars,
        (logdecay_t, queries, keys, values, grad),
        [((512, 8), F32), ((8, 512), F32), MESSAGE, MESSAGE, held, held, held, HALF, HALF],
        after,
        far=(1, 2, 3, 4),
        scratch=[pltpu.SemaphoreType.DMA((11,))],
        room=48,
    )


def chip_kernel(base, s_ref, mine_ref, got_ref, out_ref):
    first = s_ref[base] == 0
    d_mine, d_got = message_decays(mine_ref), message_decays(got_ref)
    w_mine = jnp.where(first, jnp.exp(d_got), 1.0)
    w_got = jnp.where(first, 1.0, jnp.exp(d_mine))
    for i in range(4):
        rows = slice(i * 128, i * 128 + 128)
        out_ref[rows, :] = (
            w_mine[i : i + 1] * mine_ref[rows, :].astype(F32) + w_got[i : i + 1] * got_ref[rows, :].astype(F32)
        ).astype(BF16)
    out_ref[512:528, :] = pack_decays(d_mine + d_got)


def meet_kernel(slot, s_ref, mine_ref, got_ref, *refs):
    prefix_in = refs[0] if len(refs) > 3 else None
    before_in = refs[1] if len(refs) > 3 else None
    total_ref, prefix_ref, before_ref = refs[-3:]
    later = s_ref[slot] == 1
    d_mine, d_got = message_decays(mine_ref), message_decays(got_ref)
    w_mine = jnp.where(later, 1.0, jnp.exp(d_got))
    w_got = jnp.where(later, jnp.exp(d_mine), 1.0)
    before = jnp.zeros((4, 128), F32) if before_in is None else before_in[0:4, :]
    reach = jnp.where(later, jnp.exp(before), 0.0)
    for i in range(4):
        rows = slice(i * 128, i * 128 + 128)
        mine, got = mine_ref[rows, :].astype(F32), got_ref[rows, :].astype(F32)
        total_ref[rows, :] = (w_mine[i : i + 1] * mine + w_got[i : i + 1] * got).astype(BF16)
        prefix = reach[i : i + 1] * got
        prefix_ref[rows, :] = prefix if prefix_in is None else prefix_in[rows, :] + prefix
    total_ref[512:528, :] = pack_decays(d_mine + d_got)
    before = before + jnp.where(later, d_got, 0.0)
    before_ref[...] = jnp.concatenate([before, before], axis=0)


def arrive_kernel(base, s_ref, last_ref, prefix_ref, before_ref, mine_ref, got_ref, keep_ref, send_ref):
    first = s_ref[base] == 0
    later = s_ref[base + 4] == 1
    reach = jnp.where(later, jnp.exp(before_ref[0:4, :]), 0.0)
    d_first = jnp.where(first, message_decays(mine_ref), message_decays(got_ref))
    w_first = jnp.exp(d_first)
    for i in range(4):
        rows = slice(i * 128, i * 128 + 128)
        at_first = prefix_ref[rows, :] + reach[i : i + 1] * last_ref[rows, :].astype(F32)
        state_first = jnp.where(first, mine_ref[rows, :].astype(F32), got_ref[rows, :].astype(F32))
        at_second = w_first[i : i + 1] * at_first + state_first
        keep_ref[rows, :] = jnp.where(first, at_first, at_second).astype(BF16)
        send_ref[rows, :] = jnp.where(first, at_second, at_first).astype(BF16)


SWAP = [(i, i ^ 1) for i in range(32)]
MEETINGS = [[(i, i ^ far) for i in range(32)] for far in (2, 4, 8, 16)]


def scan_blocks(scalars, mine, send, base, beside):
    got = lax.ppermute(send, "seq", SWAP)
    (total,) = call(functools.partial(chip_kernel, base), "chip_total", scalars, (mine, got), [MESSAGE])
    held = ()
    after = (total,)
    for turn in range(3):
        met = lax.ppermute(total, "seq", MEETINGS[turn])
        after = beside[turn](after)
        held = call(
            functools.partial(meet_kernel, base + 1 + turn),
            "meet",
            scalars,
            (total, met, *held),
            [MESSAGE, ((512, 128), F32), ((8, 128), F32)],
            after,
        )
        total, held = held[0], held[1:]
        after = (held[1],)
    met = lax.ppermute(total, "seq", MEETINGS[3])
    after = beside[3](after)
    keep, send_back = call(
        functools.partial(arrive_kernel, base),
        "arrive",
        scalars,
        (met, *held, mine, got),
        [STATES, STATES],
        after,
    )
    return keep, lax.ppermute(send_back, "seq", SWAP)


def decay_block(cum, cum_t, head, low, high):
    diff = cum[low:high, head : head + 1] - cum_t[head : head + 1, :high]
    rows = lax.broadcasted_iota(jnp.int32, diff.shape, 0) + low
    cols = lax.broadcasted_iota(jnp.int32, diff.shape, 1)
    return jnp.exp(jnp.where(rows >= cols, diff, -1e30))


def local_kernel(s_ref, cum_ref, cumt_ref, q_ref, k_ref, v_ref, w_hbm, out_ref, scaled_ref, turned_ref, w_ref, sems):
    loads = []
    for part in range(4):
        rows = slice(part * 256, part * 256 + 256)
        loads.append(pltpu.make_async_copy(w_hbm.at[rows, :], w_ref.at[rows, :], sems.at[part]))
        loads[-1].start()
    cum, cum_t = cum_ref[...], cumt_ref[...]
    rise = jnp.exp(cum)
    for head in range(8):
        at = head_columns(head)
        scaled = q_ref[:, at].astype(F32) * rise[:, head : head + 1]
        scaled_ref[:, at] = scaled.astype(BF16)
        turned_ref[at, :] = scaled.T.astype(BF16)
        for low in (0, 256):
            high = low + 256
            table = decay_block(cum, cum_t, head, low, high)
            probs = (dot(q_ref[low:high, at], k_ref[:high, at], NT) * table).astype(BF16)
            out_ref[low:high, at] = dot(probs, v_ref[:high, at])
    for copy in loads:
        copy.wait()


def local(scalars, cum, cum_t, q, k, v, weight, after):
    return call(
        local_kernel,
        "local",
        scalars,
        (cum, cum_t, q, k, v, weight),
        [((512, 1024), F32), ((512, 1024), BF16), ((1024, 512), BF16), ((1024, 6144), BF16)],
        after,
        far=(5,),
        room=34,
        scratch=[pltpu.SemaphoreType.DMA((4,))],
    )


def arrived(s_ref, head, keep_ref, got_ref):
    rows = slice(head % 4 * 128, head % 4 * 128 + 128)
    return jnp.where(s_ref[CORE] == head // 4, keep_ref[rows, :], got_ref[rows, :])


def attend_kernel(s_ref, local_ref, scaled_ref, keep_ref, got_ref, normed_ref, unit_ref, scale_ref):
    for head in range(8):
        at = head_columns(head)
        att = local_ref[:, at] + dot(scaled_ref[:, at], arrived(s_ref, head, keep_ref, got_ref))
        scale = lax.rsqrt(jnp.mean(att * att, axis=1, keepdims=True) + EPS)
        unit = att * scale
        unit_ref[:, at] = unit
        scale_ref[:, at] = jnp.broadcast_to(scale, unit.shape)
        normed_ref[:, at] = unit.astype(BF16)


WHOLE = ((512, 1536), BF16)
WIDE_HALF = ((256, 1536), F32)


OWN, NEAR_LEFT, NEAR_RIGHT, FAR, CORE = 10, 11, 12, 13, 14


def block_columns(s_ref, slot, offset=0, size=1536):
    return pl.ds(pl.multiple_of(s_ref[slot] * 1536 + offset, 128), size)


def products(s_ref, x_ref, w_ref, slot, top_ref, bottom_ref):
    for offset in (0, 512, 1024):
        out = dot(x_ref[...], w_ref[:, block_columns(s_ref, slot, offset, 512)])
        at = slice(offset, offset + 512)
        top_ref[:, at] = out[:256].astype(top_ref.dtype)
        bottom_ref[:, at] = out[256:].astype(bottom_ref.dtype)


def project_near_kernel(s_ref, x_ref, w_ref, right_top, right_bottom, left_top, left_bottom):
    products(s_ref, x_ref, w_ref, NEAR_RIGHT, right_top, right_bottom)
    products(s_ref, x_ref, w_ref, NEAR_LEFT, left_top, left_bottom)


def project_one_kernel(slot, s_ref, x_ref, w_ref, top_ref, bottom_ref):
    products(s_ref, x_ref, w_ref, slot, top_ref, bottom_ref)


def halves_kernel(s_ref, grad_hbm, top_ref, bottom_ref, order_ref, sems):
    order_ref[...] = jnp.zeros((8, 128), F32)
    copies = [
        pltpu.make_async_copy(grad_hbm.at[:256, :], top_ref, sems.at[0]),
        pltpu.make_async_copy(grad_hbm.at[256:, :], bottom_ref, sems.at[1]),
    ]
    for copy in copies:
        copy.start()
    for copy in copies:
        copy.wait()


def split_kernel(s_ref, a_ref, b_ref, top_ref, bottom_ref):
    top_ref[...] = a_ref[...]
    bottom_ref[...] = b_ref[...]


def join_kernel(s_ref, right_ref, from_left, left_ref, from_right, out_right, out_left):
    out_right[...] = (right_ref[...] + from_left[...].astype(F32)).astype(BF16)
    out_left[...] = (left_ref[...] + from_right[...].astype(F32)).astype(BF16)


def add_direct_kernel(s_ref, top_ref, bottom_ref, from_right, from_left, top_out, bottom_out):
    top_out[...] = top_ref[...] + from_right[...].astype(F32)
    bottom_out[...] = bottom_ref[...] + from_left[...].astype(F32)


def total_kernel(s_ref, top_ref, bottom_ref, from_left, from_right, out_ref, out_held, sems):
    copies = []
    for i, (own_ref, a_ref) in enumerate(((top_ref, from_left), (bottom_ref, from_right))):
        for j in range(2):
            rows = slice(j * 128, j * 128 + 128)
            here = slice(i * 256 + j * 128, i * 256 + j * 128 + 128)
            total = own_ref[rows, :] + a_ref[rows, :].astype(F32)
            out_held[here, :] = total.astype(BF16)
            copies.append(pltpu.make_async_copy(out_held.at[here, :], out_ref.at[here, :], sems.at[i * 2 + j]))
            copies[-1].start()
    for copy in copies:
        copy.wait()


def grad_own_kernel(s_ref, x_ref, w_ref, out_ref):
    for low in range(0, 1024, 256):
        rows = slice(low, low + 256)
        out_ref[:, rows] = dot(x_ref[...], w_ref[rows, block_columns(s_ref, OWN)], NT)


def grad_near_kernel(s_ref, a_top, a_bottom, b_top, b_bottom, w_ref, acc_ref, out_ref):
    a = jnp.concatenate([a_top[...], a_bottom[...]], axis=0)
    b = jnp.concatenate([b_top[...], b_bottom[...]], axis=0)
    for low in range(0, 1024, 256):
        rows = slice(low, low + 256)
        out_ref[:, rows] = (
            acc_ref[:, rows]
            + dot(a, w_ref[rows, block_columns(s_ref, NEAR_LEFT)], NT)
            + dot(b, w_ref[rows, block_columns(s_ref, NEAR_RIGHT)], NT)
        )


def grad_far_kernel(
    s_ref, c_ref, d_ref, w_ref, acc_ref, unit_ref, scale_ref, turned_ref, cumt_ref, grad_ref, mine_ref, send_ref
):
    core = s_ref[CORE]
    x = jnp.concatenate([c_ref[...], d_ref[...]], axis=0)
    for low in range(0, 1024, 256):
        rows = slice(low, low + 256)
        acc = acc_ref[:, rows] + dot(x, w_ref[rows, block_columns(s_ref, FAR)], NT)
        for i in range(2):
            head = low // 128 + i
            at = head_columns(head)
            unit, grad = unit_ref[:, at], acc[:, i * 128 : i * 128 + 128]
            along = jnp.mean(grad * unit, axis=1, keepdims=True)
            out = (scale_ref[:, at] * (grad - unit * along)).astype(BF16)
            grad_ref[:, at] = out
            put_state(core, head, dot(turned_ref[at, :], out).astype(BF16), mine_ref, send_ref)
    put_decays(core, cumt_ref[...], mine_ref, send_ref)


def inside_kernel(heads, s_ref, cum_ref, cumt_ref, q_ref, k_ref, v_ref, g_ref, keep_ref, got_ref, *refs):
    gq_ref, gk_ref, gv_ref = refs[-3:]
    cum, cum_t = cum_ref[...], cumt_ref[...]
    rise = jnp.exp(cum)
    if len(refs) > 3:
        gq_ref[:, :512] = refs[0][...]
    for head in heads:
        at = head_columns(head)
        to = head_columns(head - heads[0])
        to_q = at if len(refs) > 3 else to
        incoming = arrived(s_ref, head, keep_ref, got_ref)
        early_k = early_v = None
        for low in (0, 256):
            high = low + 256
            q, g = q_ref[low:high, at], g_ref[low:high, at]
            k, v = k_ref[:high, at], v_ref[:high, at]
            table = decay_block(cum, cum_t, head, low, high)
            probs = (dot(q, k, NT) * table).astype(BF16)
            scores = (dot(g, v, NT) * table).astype(BF16)
            gq = dot(scores, k) + rise[low:high, head : head + 1] * dot(g, incoming, NT)
            gq_ref[low:high, to_q] = gq.astype(BF16)
            part_k, part_v = dot(scores, q, TN), dot(probs, g, TN)
            if low == 0:
                early_k, early_v = part_k, part_v
            else:
                gk_ref[:256, to] = early_k + part_k[:256]
                gk_ref[256:, to] = part_k[256:]
                gv_ref[:256, to] = early_v + part_v[:256]
                gv_ref[256:, to] = part_v[256:]


def finish_kernel(
    s_ref, cum_ref, k_ref, v_ref, gk_a, gv_a, gk_b, gv_b, keep_ref, got_ref, gk_out, gv_out, order_ref, gk_held, gv_held, sems
):
    cum = cum_ref[...]
    fall = jnp.exp(cum[511:512, :] - cum)
    copies = []
    for head in range(8):
        at, part = head_columns(head), head_columns(head % 4)
        gk_ref, gv_ref = ((gk_a, gv_a), (gk_b, gv_b))[head // 4]
        outgoing = arrived(s_ref, head, keep_ref, got_ref)
        factor = fall[:, head : head + 1]
        gk_held[:, at] = (gk_ref[:, part] + factor * dot(v_ref[:, at], outgoing, NT)).astype(BF16)
        gv_held[:, at] = (gv_ref[:, part] + factor * dot(k_ref[:, at], outgoing)).astype(BF16)
        if head % 2 == 1:
            done = slice(head * 128 - 128, head * 128 + 128)
            for i, (held, out) in enumerate(((gk_held, gk_out), (gv_held, gv_out))):
                copies.append(pltpu.make_async_copy(held.at[:, done], out.at[:, done], sems.at[head - 1 + i]))
                copies[-1].start()
    order_ref[...] = jnp.zeros((8, 128), F32)
    for copy in copies:
        copy.wait()


RIGHT = [(i, (i + 1) % 4) for i in range(4)]
LEFT = [(i, (i + 3) % 4) for i in range(4)]


def body(queries, keys, values, logdecay, weight, output_gradient):
    at = lax.axis_index("seq").astype(jnp.int32)
    h = lax.axis_index("head").astype(jnp.int32)
    core, x, z = at % 2, at // 2 % 4, at // 8
    places = [core, x % 2, x // 2, z % 2, z // 2]
    blocks = [h, (h + 3) % 4, (h + 1) % 4, (h + 2) % 4, core]
    scalars = jnp.stack(places + [1 - place for place in places] + blocks).astype(jnp.int32)

    right = lambda a: lax.ppermute(a, "head", RIGHT)
    left = lambda a: lax.ppermute(a, "head", LEFT)
    wide, narrow = ((512, 1024), F32), ((512, 1024), BF16)

    top, bottom, order = call(
        halves_kernel,
        "halves",
        None,
        (output_gradient,),
        [HALF, HALF, ((8, 128), F32)],
        far=(0,),
        scratch=[pltpu.SemaphoreType.DMA((2,))],
        room=52,
    )
    a_top, b_bottom = right(top), left(bottom)
    cum, cum_t, mine, send, q, k, v, top, bottom = own_states(
        scalars, logdecay.T, queries, keys, values, output_gradient, (order,)
    )
    a_bottom, b_top = right(bottom), left(top)
    made = {}

    def make_local(after):
        made["local"] = local(scalars, cum, cum_t, q, k, v, weight, after)
        return made["local"][:1]

    def make_grad_own(after):
        w = made["local"][3]
        made["acc"] = call(grad_own_kernel, "grad_own", scalars, (output_gradient, w), [wide], after)[0]
        return (made["acc"],)

    def make_split(after):
        made["split"] = call(split_kernel, "split", None, (a_top, b_bottom), [HALF, HALF], after)
        return made["split"][:1]

    keep, got = scan_blocks(scalars, mine, send, 0, (make_local, make_grad_own, make_split, lambda after: after))
    local_part, scaled, turned, w = made["local"]
    acc = made["acc"]
    c, d = right(made["split"][0]), left(made["split"][1])
    normed, unit, scale = call(
        attend_kernel, "attend", scalars, (local_part, scaled, keep, got), [narrow, wide, wide]
    )

    (acc,) = call(grad_near_kernel, "grad_near", scalars, (a_top, a_bottom, b_top, b_bottom, w, acc), [wide], (unit,))
    far = call(functools.partial(project_one_kernel, FAR), "project_far", scalars, (normed, w), [HALF] * 2, (acc,))
    from_left, from_right = right(far[0]), left(far[1])
    near = call(
        project_near_kernel, "project_near", scalars, (normed, w), [WIDE_HALF, HALF, HALF, WIDE_HALF], far[:1]
    )
    grad, mine_g, send_g = call(
        grad_far_kernel,
        "grad_far",
        scalars,
        (c, d, w, acc, unit, scale, turned, cum_t),
        [narrow, MESSAGE, MESSAGE],
        near[:1],
    )
    inputs = (cum, cum_t, q, k, v, grad, keep, got)
    right_top, right_bottom, left_top, left_bottom = near
    direct_r, direct_l = right(right_bottom), left(left_top)

    def inside_first(after):
        made["a"] = call(
            functools.partial(inside_kernel, range(0, 4)),
            "inside",
            scalars,
            inputs,
            [((512, 512), BF16), ((512, 512), F32), ((512, 512), F32)],
            after,
        )
        return made["a"][:1]

    def inside_second(after):
        made["b"] = call(
            functools.partial(inside_kernel, range(4, 8)),
            "inside",
            scalars,
            inputs + (made["a"][0],),
            [narrow, ((512, 512), F32), ((512, 512), F32)],
            after,
        )
        return made["b"][1:2]

    def join(after):
        parts = (right_top, from_left, left_bottom, from_right)
        made["joined"] = call(join_kernel, "join", None, parts, [HALF, HALF], after)
        return made["joined"][:1]

    def project_own(after):
        one = functools.partial(project_one_kernel, OWN)
        made["own"] = call(one, "project_own", scalars, (normed, w), [WIDE_HALF] * 2, after)
        return made["own"][:1]

    def add_direct(after):
        parts = (*made["own"], direct_l, direct_r)
        made["own"] = call(add_direct_kernel, "add_direct", None, parts, [WIDE_HALF] * 2, after)
        return made["own"][:1]

    turns = (
        inside_first,
        lambda after: project_own(join(after)),
        lambda after: add_direct(inside_second(after)),
        lambda after: after,
    )
    keep_g, got_g = scan_blocks(scalars, mine_g, send_g, 5, turns)
    joined_r, joined_l = right(made["joined"][0]), left(made["joined"][1])
    gq = made["b"][0]
    gk, gv, order = call(
        finish_kernel,
        "finish",
        scalars,
        (cum, k, v, *made["a"][1:], *made["b"][1:], keep_g, got_g),
        [narrow, narrow, ((8, 128), F32)],
        far_outs=(0, 1),
        scratch=[pltpu.VMEM((512, 1024), BF16), pltpu.VMEM((512, 1024), BF16), pltpu.SemaphoreType.DMA((8,))],
    )
    (out,) = call(
        total_kernel,
        "total",
        None,
        (*made["own"], joined_r, joined_l),
        [WHOLE],
        (order,),
        far_outs=(0,),
        scratch=[pltpu.VMEM((512, 1536), BF16), pltpu.SemaphoreType.DMA((4,))],
    )
    return out, gq, gk, gv


def solution(mesh):
    return jax.shard_map(
        body,
        mesh=mesh,
        in_specs=(
            P("seq", "head"),
            P("seq", "head"),
            P("seq", "head"),
            P("seq", "head"),
            P("head", None),
            P("seq", "head"),
        ),
        out_specs=(P("seq", "head"), P("seq", "head"), P("seq", "head"), P("seq", "head")),
        check_vma=False,
    )
```

```python
import functools

import jax
import jax.numpy as jnp
from jax import lax
from jax.experimental import pallas as pl
from jax.experimental.pallas import tpu as pltpu
from jax.sharding import PartitionSpec as P

EPS = 1e-05
F32 = jnp.float32
BF16 = jnp.bfloat16
MIB = 1024 * 1024
GIGA = 10**9

NN = (((1,), (0,)), ((), ()))
NT = (((1,), (1,)), ((), ()))
TN = (((0,), (0,)), ((), ()))


def dot(left, right, form=NN):
    return lax.dot_general(left, right, form, preferred_element_type=F32)


VMEM = pl.BlockSpec(memory_space=pltpu.VMEM)
SMEM = pl.BlockSpec(memory_space=pltpu.SMEM)
ANY = pl.BlockSpec(memory_space=pl.ANY)
HBM = pl.BlockSpec(memory_space=pltpu.HBM)


COST = dict(
    own_states=8 * GIGA,
    chip_total=0,
    local=0,
    meet=0,
    grad_own=0,
    arrive=0,
    split=0,
    halves=0,
    attend=0,
    grad_near=0,
    project_far=0,
    project_near=0,
    project_own=0,
    grad_far=0,
    join=0,
    add_direct=0,
    inside=0,
    finish=0,
    total=0,
)


def call(kernel, name, scalars, args, outs, after=(), far=(), far_outs=(), scratch=(), room=12):
    count, waits = len(args), len(after)
    lead = () if scalars is None else (scalars,)

    def run(*refs):
        refs = refs if lead else (None, *refs)
        kernel(*refs[: 1 + count], *refs[1 + count + waits :])

    return pl.pallas_call(
        run,
        out_shape=[jax.ShapeDtypeStruct(shape, dtype) for shape, dtype in outs],
        in_specs=[SMEM] * len(lead) + [HBM if i in far else VMEM for i in range(count)] + [ANY] * waits,
        out_specs=[HBM if i in far_outs else VMEM for i in range(len(outs))],
        scratch_shapes=list(scratch),
        compiler_params=pltpu.CompilerParams(vmem_limit_bytes=room * MIB),
        cost_estimate=pl.CostEstimate(flops=COST[name], bytes_accessed=0, transcendentals=0),
        name=name,
    )(*lead, *args, *after)


def three_terms(x):
    high = x.astype(BF16)
    rest = x - high.astype(F32)
    middle = rest.astype(BF16)
    low = (rest - middle.astype(F32)).astype(BF16)
    return high, middle, low


def head_columns(head):
    return slice(head * 128, head * 128 + 128)


def pack_decays(decays):
    high, middle, low = three_terms(decays)
    rows = [t.astype(F32) for t in (high, middle, low)]
    return jnp.concatenate(rows + [jnp.zeros_like(decays)], axis=0).astype(BF16)


def message_decays(ref):
    rows = ref[512:528, :].astype(F32)
    return rows[0:4] + rows[4:8] + rows[8:12]


MESSAGE = ((528, 128), BF16)
STATES = ((512, 128), BF16)
HALF = ((256, 1536), BF16)


def put_state(core, head, state, mine_ref, send_ref):
    rows = slice(head % 4 * 128, head % 4 * 128 + 128)
    here = core == head // 4

    @pl.when(here)
    def _():
        mine_ref[rows, :] = state

    @pl.when(jnp.logical_not(here))
    def _():
        send_ref[rows, :] = state


def put_decays(core, cum_t, mine_ref, send_ref):
    last = jnp.broadcast_to(cum_t[:, 511:512], (8, 128))
    swap = core == 1
    mine_ref[512:528, :] = pack_decays(jnp.where(swap, last[4:8], last[0:4]))
    send_ref[512:528, :] = pack_decays(jnp.where(swap, last[0:4], last[4:8]))


def state_kernel(
    s_ref,
    ld_ref,
    q_hbm,
    k_hbm,
    v_hbm,
    grad_hbm,
    cum_ref,
    cumt_ref,
    mine_ref,
    send_ref,
    q_ref,
    k_ref,
    v_ref,
    top_ref,
    bottom_ref,
    sems,
):
    core = s_ref[CORE]
    loads = []
    for part in range(4):
        cols = slice(part * 256, part * 256 + 256)
        pair = [
            pltpu.make_async_copy(far.at[:, cols], near.at[:, cols], sems.at[part * 2 + i])
            for i, (far, near) in enumerate(((k_hbm, k_ref), (v_hbm, v_ref)))
        ]
        for copy in pair:
            copy.start()
        loads.append(pair)
    late = [
        pltpu.make_async_copy(q_hbm, q_ref, sems.at[8]),
        pltpu.make_async_copy(grad_hbm.at[:256, :], top_ref, sems.at[9]),
        pltpu.make_async_copy(grad_hbm.at[256:, :], bottom_ref, sems.at[10]),
    ]
    for copy in late:
        copy.start()

    rows = lax.broadcasted_iota(jnp.int32, (512, 512), 0)
    cols = lax.broadcasted_iota(jnp.int32, (512, 512), 1)
    upper = jnp.where(rows <= cols, 1.0, 0.0).astype(BF16)
    lower = jnp.where(rows >= cols, 1.0, 0.0).astype(BF16)
    cum = jnp.zeros((512, 8), F32)
    cum_t = jnp.zeros((8, 512), F32)
    for term in three_terms(ld_ref[...])[::-1]:
        cum = cum + dot(lower, term, NT)
        cum_t = cum_t + dot(term, upper)
    cum_ref[...] = cum
    cumt_ref[...] = cum_t
    fall = jnp.exp(cum[511:512, :] - cum)
    for head in range(8):
        if head % 2 == 0:
            for copy in loads[head // 2]:
                copy.wait()
        at = head_columns(head)
        faded = (k_ref[:, at].astype(F32) * fall[:, head : head + 1]).astype(BF16)
        put_state(core, head, dot(faded, v_ref[:, at], TN).astype(BF16), mine_ref, send_ref)
    put_decays(core, cum_t, mine_ref, send_ref)
    for copy in late:
        copy.wait()


def own_states(scalars, logdecay_t, queries, keys, values, grad, after):
    held = ((512, 1024), BF16)
    return call(
        state_kernel,
        "own_states",
        scalars,
        (logdecay_t, queries, keys, values, grad),
        [((512, 8), F32), ((8, 512), F32), MESSAGE, MESSAGE, held, held, held, HALF, HALF],
        after,
        far=(1, 2, 3, 4),
        scratch=[pltpu.SemaphoreType.DMA((11,))],
        room=48,
    )


def chip_kernel(base, s_ref, mine_ref, got_ref, out_ref):
    first = s_ref[base] == 0
    d_mine, d_got = message_decays(mine_ref), message_decays(got_ref)
    w_mine = jnp.where(first, jnp.exp(d_got), 1.0)
    w_got = jnp.where(first, 1.0, jnp.exp(d_mine))
    for i in range(4):
        rows = slice(i * 128, i * 128 + 128)
        out_ref[rows, :] = (
            w_mine[i : i + 1] * mine_ref[rows, :].astype(F32) + w_got[i : i + 1] * got_ref[rows, :].astype(F32)
        ).astype(BF16)
    out_ref[512:528, :] = pack_decays(d_mine + d_got)


def meet_kernel(slot, s_ref, mine_ref, got_ref, *refs):
    prefix_in = refs[0] if len(refs) > 3 else None
    before_in = refs[1] if len(refs) > 3 else None
    total_ref, prefix_ref, before_ref = refs[-3:]
    later = s_ref[slot] == 1
    d_mine, d_got = message_decays(mine_ref), message_decays(got_ref)
    w_mine = jnp.where(later, 1.0, jnp.exp(d_got))
    w_got = jnp.where(later, jnp.exp(d_mine), 1.0)
    before = jnp.zeros((4, 128), F32) if before_in is None else before_in[0:4, :]
    reach = jnp.where(later, jnp.exp(before), 0.0)
    for i in range(4):
        rows = slice(i * 128, i * 128 + 128)
        mine, got = mine_ref[rows, :].astype(F32), got_ref[rows, :].astype(F32)
        total_ref[rows, :] = (w_mine[i : i + 1] * mine + w_got[i : i + 1] * got).astype(BF16)
        prefix = reach[i : i + 1] * got
        prefix_ref[rows, :] = prefix if prefix_in is None else prefix_in[rows, :] + prefix
    total_ref[512:528, :] = pack_decays(d_mine + d_got)
    before = before + jnp.where(later, d_got, 0.0)
    before_ref[...] = jnp.concatenate([before, before], axis=0)


def arrive_kernel(base, s_ref, last_ref, prefix_ref, before_ref, mine_ref, got_ref, keep_ref, send_ref):
    first = s_ref[base] == 0
    later = s_ref[base + 4] == 1
    reach = jnp.where(later, jnp.exp(before_ref[0:4, :]), 0.0)
    d_first = jnp.where(first, message_decays(mine_ref), message_decays(got_ref))
    w_first = jnp.exp(d_first)
    for i in range(4):
        rows = slice(i * 128, i * 128 + 128)
        at_first = prefix_ref[rows, :] + reach[i : i + 1] * last_ref[rows, :].astype(F32)
        state_first = jnp.where(first, mine_ref[rows, :].astype(F32), got_ref[rows, :].astype(F32))
        at_second = w_first[i : i + 1] * at_first + state_first
        keep_ref[rows, :] = jnp.where(first, at_first, at_second).astype(BF16)
        send_ref[rows, :] = jnp.where(first, at_second, at_first).astype(BF16)


SWAP = [(i, i ^ 1) for i in range(32)]
MEETINGS = [[(i, i ^ far) for i in range(32)] for far in (2, 4, 8, 16)]


def scan_blocks(scalars, mine, send, base, beside):
    got = lax.ppermute(send, "seq", SWAP)
    (total,) = call(functools.partial(chip_kernel, base), "chip_total", scalars, (mine, got), [MESSAGE])
    held = ()
    after = (total,)
    for turn in range(3):
        met = lax.ppermute(total, "seq", MEETINGS[turn])
        after = beside[turn](after)
        held = call(
            functools.partial(meet_kernel, base + 1 + turn),
            "meet",
            scalars,
            (total, met, *held),
            [MESSAGE, ((512, 128), F32), ((8, 128), F32)],
            after,
        )
        total, held = held[0], held[1:]
        after = (held[1],)
    met = lax.ppermute(total, "seq", MEETINGS[3])
    after = beside[3](after)
    keep, send_back = call(
        functools.partial(arrive_kernel, base),
        "arrive",
        scalars,
        (met, *held, mine, got),
        [STATES, STATES],
        after,
    )
    return keep, lax.ppermute(send_back, "seq", SWAP)


def decay_block(cum, cum_t, head, low, high):
    diff = cum[low:high, head : head + 1] - cum_t[head : head + 1, :high]
    rows = lax.broadcasted_iota(jnp.int32, diff.shape, 0) + low
    cols = lax.broadcasted_iota(jnp.int32, diff.shape, 1)
    return jnp.exp(jnp.where(rows >= cols, diff, -1e30))


def local_kernel(s_ref, cum_ref, cumt_ref, q_ref, k_ref, v_ref, w_hbm, out_ref, scaled_ref, turned_ref, w_ref, sems):
    loads = []
    for part in range(4):
        rows = slice(part * 256, part * 256 + 256)
        loads.append(pltpu.make_async_copy(w_hbm.at[rows, :], w_ref.at[rows, :], sems.at[part]))
        loads[-1].start()
    cum, cum_t = cum_ref[...], cumt_ref[...]
    rise = jnp.exp(cum)
    for head in range(8):
        at = head_columns(head)
        scaled = q_ref[:, at].astype(F32) * rise[:, head : head + 1]
        scaled_ref[:, at] = scaled.astype(BF16)
        turned_ref[at, :] = scaled.T.astype(BF16)
        for low in (0, 256):
            high = low + 256
            table = decay_block(cum, cum_t, head, low, high)
            probs = (dot(q_ref[low:high, at], k_ref[:high, at], NT) * table).astype(BF16)
            out_ref[low:high, at] = dot(probs, v_ref[:high, at])
    for copy in loads:
        copy.wait()


def local(scalars, cum, cum_t, q, k, v, weight, after):
    return call(
        local_kernel,
        "local",
        scalars,
        (cum, cum_t, q, k, v, weight),
        [((512, 1024), F32), ((512, 1024), BF16), ((1024, 512), BF16), ((1024, 6144), BF16)],
        after,
        far=(5,),
        room=34,
        scratch=[pltpu.SemaphoreType.DMA((4,))],
    )


def arrived(s_ref, head, keep_ref, got_ref):
    rows = slice(head % 4 * 128, head % 4 * 128 + 128)
    return jnp.where(s_ref[CORE] == head // 4, keep_ref[rows, :], got_ref[rows, :])


def attend_kernel(s_ref, local_ref, scaled_ref, keep_ref, got_ref, normed_ref, unit_ref, scale_ref):
    for head in range(8):
        at = head_columns(head)
        att = local_ref[:, at] + dot(scaled_ref[:, at], arrived(s_ref, head, keep_ref, got_ref))
        scale = lax.rsqrt(jnp.mean(att * att, axis=1, keepdims=True) + EPS)
        unit = att * scale
        unit_ref[:, at] = unit
        scale_ref[:, at] = jnp.broadcast_to(scale, unit.shape)
        normed_ref[:, at] = unit.astype(BF16)


WHOLE = ((512, 1536), BF16)
WIDE_HALF = ((256, 1536), F32)


OWN, NEAR_LEFT, NEAR_RIGHT, FAR, CORE = 10, 11, 12, 13, 14


def block_columns(s_ref, slot, offset=0, size=1536):
    return pl.ds(pl.multiple_of(s_ref[slot] * 1536 + offset, 128), size)


def products(s_ref, x_ref, w_ref, slot, top_ref, bottom_ref):
    for offset in (0, 512, 1024):
        out = dot(x_ref[...], w_ref[:, block_columns(s_ref, slot, offset, 512)])
        at = slice(offset, offset + 512)
        top_ref[:, at] = out[:256].astype(top_ref.dtype)
        bottom_ref[:, at] = out[256:].astype(bottom_ref.dtype)


def project_near_kernel(s_ref, x_ref, w_ref, right_top, right_bottom, left_top, left_bottom):
    products(s_ref, x_ref, w_ref, NEAR_RIGHT, right_top, right_bottom)
    products(s_ref, x_ref, w_ref, NEAR_LEFT, left_top, left_bottom)


def project_one_kernel(slot, s_ref, x_ref, w_ref, top_ref, bottom_ref):
    products(s_ref, x_ref, w_ref, slot, top_ref, bottom_ref)


def halves_kernel(s_ref, grad_hbm, top_ref, bottom_ref, order_ref, sems):
    order_ref[...] = jnp.zeros((8, 128), F32)
    copies = [
        pltpu.make_async_copy(grad_hbm.at[:256, :], top_ref, sems.at[0]),
        pltpu.make_async_copy(grad_hbm.at[256:, :], bottom_ref, sems.at[1]),
    ]
    for copy in copies:
        copy.start()
    for copy in copies:
        copy.wait()


def split_kernel(s_ref, a_ref, b_ref, top_ref, bottom_ref):
    top_ref[...] = a_ref[...]
    bottom_ref[...] = b_ref[...]


def join_kernel(s_ref, right_ref, from_left, left_ref, from_right, out_right, out_left):
    out_right[...] = (right_ref[...] + from_left[...].astype(F32)).astype(BF16)
    out_left[...] = (left_ref[...] + from_right[...].astype(F32)).astype(BF16)


def add_direct_kernel(s_ref, top_ref, bottom_ref, from_right, from_left, top_out, bottom_out):
    top_out[...] = top_ref[...] + from_right[...].astype(F32)
    bottom_out[...] = bottom_ref[...] + from_left[...].astype(F32)


def total_kernel(s_ref, top_ref, bottom_ref, from_left, from_right, out_ref, out_held, sems):
    copies = []
    for i, (own_ref, a_ref) in enumerate(((top_ref, from_left), (bottom_ref, from_right))):
        for j in range(2):
            rows = slice(j * 128, j * 128 + 128)
            here = slice(i * 256 + j * 128, i * 256 + j * 128 + 128)
            total = own_ref[rows, :] + a_ref[rows, :].astype(F32)
            out_held[here, :] = total.astype(BF16)
            copies.append(pltpu.make_async_copy(out_held.at[here, :], out_ref.at[here, :], sems.at[i * 2 + j]))
            copies[-1].start()
    for copy in copies:
        copy.wait()


def grad_own_kernel(s_ref, x_ref, w_ref, out_ref):
    for low in range(0, 1024, 256):
        rows = slice(low, low + 256)
        out_ref[:, rows] = dot(x_ref[...], w_ref[rows, block_columns(s_ref, OWN)], NT)


def grad_near_kernel(s_ref, a_top, a_bottom, b_top, b_bottom, w_ref, acc_ref, out_ref):
    a = jnp.concatenate([a_top[...], a_bottom[...]], axis=0)
    b = jnp.concatenate([b_top[...], b_bottom[...]], axis=0)
    for low in range(0, 1024, 256):
        rows = slice(low, low + 256)
        out_ref[:, rows] = (
            acc_ref[:, rows]
            + dot(a, w_ref[rows, block_columns(s_ref, NEAR_LEFT)], NT)
            + dot(b, w_ref[rows, block_columns(s_ref, NEAR_RIGHT)], NT)
        )


def grad_far_kernel(
    s_ref, c_ref, d_ref, w_ref, acc_ref, unit_ref, scale_ref, turned_ref, cumt_ref, grad_ref, mine_ref, send_ref
):
    core = s_ref[CORE]
    x = jnp.concatenate([c_ref[...], d_ref[...]], axis=0)
    for low in range(0, 1024, 256):
        rows = slice(low, low + 256)
        acc = acc_ref[:, rows] + dot(x, w_ref[rows, block_columns(s_ref, FAR)], NT)
        for i in range(2):
            head = low // 128 + i
            at = head_columns(head)
            unit, grad = unit_ref[:, at], acc[:, i * 128 : i * 128 + 128]
            along = jnp.mean(grad * unit, axis=1, keepdims=True)
            out = (scale_ref[:, at] * (grad - unit * along)).astype(BF16)
            grad_ref[:, at] = out
            put_state(core, head, dot(turned_ref[at, :], out).astype(BF16), mine_ref, send_ref)
    put_decays(core, cumt_ref[...], mine_ref, send_ref)


def inside_kernel(heads, s_ref, cum_ref, cumt_ref, q_ref, k_ref, v_ref, g_ref, keep_ref, got_ref, *refs):
    gq_ref, gk_ref, gv_ref = refs[-3:]
    cum, cum_t = cum_ref[...], cumt_ref[...]
    rise = jnp.exp(cum)
    if len(refs) > 3:
        gq_ref[:, :512] = refs[0][...]
    for head in heads:
        at = head_columns(head)
        to = head_columns(head - heads[0])
        to_q = at if len(refs) > 3 else to
        incoming = arrived(s_ref, head, keep_ref, got_ref)
        early_k = early_v = None
        for low in (0, 256):
            high = low + 256
            q, g = q_ref[low:high, at], g_ref[low:high, at]
            k, v = k_ref[:high, at], v_ref[:high, at]
            table = decay_block(cum, cum_t, head, low, high)
            probs = (dot(q, k, NT) * table).astype(BF16)
            scores = (dot(g, v, NT) * table).astype(BF16)
            gq = dot(scores, k) + rise[low:high, head : head + 1] * dot(g, incoming, NT)
            gq_ref[low:high, to_q] = gq.astype(BF16)
            part_k, part_v = dot(scores, q, TN), dot(probs, g, TN)
            if low == 0:
                early_k, early_v = part_k, part_v
            else:
                gk_ref[:256, to] = early_k + part_k[:256]
                gk_ref[256:, to] = part_k[256:]
                gv_ref[:256, to] = early_v + part_v[:256]
                gv_ref[256:, to] = part_v[256:]


def finish_kernel(
    s_ref, cum_ref, k_ref, v_ref, gk_a, gv_a, gk_b, gv_b, keep_ref, got_ref, gk_out, gv_out, order_ref, gk_held, gv_held, sems
):
    cum = cum_ref[...]
    fall = jnp.exp(cum[511:512, :] - cum)
    copies = []
    for head in range(8):
        at, part = head_columns(head), head_columns(head % 4)
        gk_ref, gv_ref = ((gk_a, gv_a), (gk_b, gv_b))[head // 4]
        outgoing = arrived(s_ref, head, keep_ref, got_ref)
        factor = fall[:, head : head + 1]
        gk_held[:, at] = (gk_ref[:, part] + factor * dot(v_ref[:, at], outgoing, NT)).astype(BF16)
        gv_held[:, at] = (gv_ref[:, part] + factor * dot(k_ref[:, at], outgoing)).astype(BF16)
        if head % 2 == 1:
            done = slice(head * 128 - 128, head * 128 + 128)
            for i, (held, out) in enumerate(((gk_held, gk_out), (gv_held, gv_out))):
                copies.append(pltpu.make_async_copy(held.at[:, done], out.at[:, done], sems.at[head - 1 + i]))
                copies[-1].start()
    order_ref[...] = jnp.zeros((8, 128), F32)
    for copy in copies:
        copy.wait()


RIGHT = [(i, (i + 1) % 4) for i in range(4)]
LEFT = [(i, (i + 3) % 4) for i in range(4)]


def body(queries, keys, values, logdecay, weight, output_gradient):
    at = lax.axis_index("seq").astype(jnp.int32)
    h = lax.axis_index("head").astype(jnp.int32)
    core, x, z = at % 2, at // 2 % 4, at // 8
    places = [core, x % 2, x // 2, z % 2, z // 2]
    blocks = [h, (h + 3) % 4, (h + 1) % 4, (h + 2) % 4, core]
    scalars = jnp.stack(places + [1 - place for place in places] + blocks).astype(jnp.int32)

    right = lambda a: lax.ppermute(a, "head", RIGHT)
    left = lambda a: lax.ppermute(a, "head", LEFT)
    wide, narrow = ((512, 1024), F32), ((512, 1024), BF16)

    top, bottom, order = call(
        halves_kernel,
        "halves",
        None,
        (output_gradient,),
        [HALF, HALF, ((8, 128), F32)],
        far=(0,),
        scratch=[pltpu.SemaphoreType.DMA((2,))],
        room=52,
    )
    a_top, b_bottom = right(top), left(bottom)
    cum, cum_t, mine, send, q, k, v, top, bottom = own_states(
        scalars, logdecay.T, queries, keys, values, output_gradient, (order,)
    )
    a_bottom, b_top = right(bottom), left(top)
    made = {}

    def make_local(after):
        made["local"] = local(scalars, cum, cum_t, q, k, v, weight, after)
        return made["local"][:1]

    def make_grad_own(after):
        w = made["local"][3]
        made["acc"] = call(grad_own_kernel, "grad_own", scalars, (output_gradient, w), [wide], after)[0]
        return (made["acc"],)

    def make_split(after):
        made["split"] = call(split_kernel, "split", None, (a_top, b_bottom), [HALF, HALF], after)
        return made["split"][:1]

    keep, got = scan_blocks(scalars, mine, send, 0, (make_local, make_grad_own, make_split, lambda after: after))
    local_part, scaled, turned, w = made["local"]
    acc = made["acc"]
    c, d = right(made["split"][0]), left(made["split"][1])
    normed, unit, scale = call(
        attend_kernel, "attend", scalars, (local_part, scaled, keep, got), [narrow, wide, wide]
    )

    (acc,) = call(grad_near_kernel, "grad_near", scalars, (a_top, a_bottom, b_top, b_bottom, w, acc), [wide], (unit,))
    far = call(functools.partial(project_one_kernel, FAR), "project_far", scalars, (normed, w), [HALF] * 2, (acc,))
    from_left, from_right = right(far[0]), left(far[1])
    near = call(
        project_near_kernel, "project_near", scalars, (normed, w), [WIDE_HALF, HALF, HALF, WIDE_HALF], far[:1]
    )
    grad, mine_g, send_g = call(
        grad_far_kernel,
        "grad_far",
        scalars,
        (c, d, w, acc, unit, scale, turned, cum_t),
        [narrow, MESSAGE, MESSAGE],
        near[:1],
    )
    inputs = (cum, cum_t, q, k, v, grad, keep, got)
    right_top, right_bottom, left_top, left_bottom = near
    direct_r, direct_l = right(right_bottom), left(left_top)

    def inside_first(after):
        made["a"] = call(
            functools.partial(inside_kernel, range(0, 4)),
            "inside",
            scalars,
            inputs,
            [((512, 512), BF16), ((512, 512), F32), ((512, 512), F32)],
            after,
        )
        return made["a"][:1]

    def inside_second(after):
        made["b"] = call(
            functools.partial(inside_kernel, range(4, 8)),
            "inside",
            scalars,
            inputs + (made["a"][0],),
            [narrow, ((512, 512), F32), ((512, 512), F32)],
            after,
        )
        return made["b"][1:2]

    def join(after):
        parts = (right_top, from_left, left_bottom, from_right)
        made["joined"] = call(join_kernel, "join", None, parts, [HALF, HALF], after)
        return made["joined"][:1]

    def project_own(after):
        one = functools.partial(project_one_kernel, OWN)
        made["own"] = call(one, "project_own", scalars, (normed, w), [WIDE_HALF] * 2, after)
        return made["own"][:1]

    def add_direct(after):
        parts = (*made["own"], direct_l, direct_r)
        made["own"] = call(add_direct_kernel, "add_direct", None, parts, [WIDE_HALF] * 2, after)
        return made["own"][:1]

    turns = (
        inside_first,
        lambda after: project_own(join(after)),
        lambda after: (*inside_second(after), direct_l, direct_r),
        add_direct,
    )
    keep_g, got_g = scan_blocks(scalars, mine_g, send_g, 5, turns)
    joined_r, joined_l = right(made["joined"][0]), left(made["joined"][1])
    gq = made["b"][0]
    gk, gv, order = call(
        finish_kernel,
        "finish",
        scalars,
        (cum, k, v, *made["a"][1:], *made["b"][1:], keep_g, got_g),
        [narrow, narrow, ((8, 128), F32)],
        far_outs=(0, 1),
        scratch=[pltpu.VMEM((512, 1024), BF16), pltpu.VMEM((512, 1024), BF16), pltpu.SemaphoreType.DMA((8,))],
    )
    (out,) = call(
        total_kernel,
        "total",
        None,
        (*made["own"], joined_r, joined_l),
        [WHOLE],
        (order,),
        far_outs=(0,),
        scratch=[pltpu.VMEM((512, 1536), BF16), pltpu.SemaphoreType.DMA((4,))],
    )
    return out, gq, gk, gv


def solution(mesh):
    return jax.shard_map(
        body,
        mesh=mesh,
        in_specs=(
            P("seq", "head"),
            P("seq", "head"),
            P("seq", "head"),
            P("seq", "head"),
            P("head", None),
            P("seq", "head"),
        ),
        out_specs=(P("seq", "head"), P("seq", "head"), P("seq", "head"), P("seq", "head")),
        check_vma=False,
    )
```
